128 devices in a mesh: feat: 8 (over x, core), dom: 16 (over y, z).
Axes of the slice: x: 4, y: 4, z: 4, core: 2. Of those that a mesh axis runs over, the one named last changes fastest.
Arguments:
- features: bfloat16 [768, 98304], P('feat', 'dom'), may hold values from -6 to 6
- adj_one: bfloat16 [768, 4, 128, 128], P('dom'), may hold values from -0.25 to 0.25
- src_one: int32 [768, 4], P('dom'), may hold values from 0 to 47
- w_self_one: bfloat16 [768, 1024], P('feat'), may hold values from -0.21875 to 0.21875
- w_neigh_one: bfloat16 [768, 1024], P('feat'), may hold values from -0.21875 to 0.21875
- bias_one: float32 [1024], replicated, may hold values from -4 to 4
- w_self_two: bfloat16 [1024, 1024], replicated, may hold values from -0.1875 to 0.1875
- w_neigh_two: bfloat16 [1024, 1024], replicated, may hold values from -0.1875 to 0.1875
- bias_two: float32 [1024], replicated, may hold values from -4 to 4
- seed_rows: int32 [16, 8, 512], P('dom', 'feat'), may hold values from 0 to 767
- adj_two: bfloat16 [16, 8, 4, 16, 128, 128], P('dom', 'feat'), may hold values from -0.125 to 0.125
- src_two: int32 [16, 8, 4, 16], P('dom', 'feat'), may hold values from 0 to 21
- send_tiles: int32 [16, 8, 4, 4], P('dom', 'feat'), may hold values from 0 to 5
- send_count: int32 [16, 8, 4], P('dom', 'feat'), may hold values from 1 to 4, as said below
- cotangent: bfloat16 [16, 4096, 1024], P('dom', 'feat'), may hold values from -6 to 6
Outputs:
- layer_two: bfloat16 [16, 4096, 1024], P('dom', 'feat')
- grad_hidden: float32 [16, 6144, 1024], P('dom', 'feat')
The draws below stay inside these ranges and needn't reach their ends.
Inputs may be any that keep to these rules, and one draw needn't show every extreme that they name: `seed_rows`: rows of the device's own block of 768 hidden rows; they may repeat. `src_one`: tiles of the same partition. `src_two`: slots of the device's source table: its 6 local tiles, then 4 slots from each of the partitions at offsets -2, -1, +1, +2; a slot beyond the sender's live count holds zeros. `send_tiles`: local tiles of the sending device; they may repeat. `send_count`: uneven over devices and directions; some device has 4 in every direction.
All inputs are finite; a program needn't handle non-finite values.
Results may differ from the reference program's by a relative error of at most 0.018.
Values may be sent and summed in bfloat16 or wider, within the bound.
No kernel may reach another device: no remote copies, remote signals or barrier semaphores. Data moves between devices by JAX's collectives and lax.ppermute only.
A program may use at most 192 MiB of HBM per device.

```python
import jax
import jax.numpy as jnp
from jax import lax

D_IN = 768
HID = 1024
TILE = 128
TILE_DEV = 6
SEED_T = 4
K1 = 4
K2 = 16
HALO_T = 4
PART_TILES = 48
PART_ROWS = 6144
ROW_DEV = 768
SEEDS_DEV = 512
NODES = 98304
N_FEAT = 8
N_DOM = 16


def draw_send_count(key, part):
    key = jax.random.fold_in(key, 7)
    count_key, row_key, col_key = jax.random.split(key, 3)
    counts = jax.random.randint(count_key, (N_DOM, N_FEAT, 4), 1, HALO_T + 1)
    row_pick = jax.random.randint(row_key, (), 0, N_DOM)
    col_pick = jax.random.randint(col_key, (), 0, N_FEAT)
    return counts.at[row_pick, col_pick, :].set(HALO_T).astype(jnp.int32)


def set_ends(drawn, own_key, least, largest):
    longest = drawn.shape.index(max(drawn.shape))
    spots = []
    for shift in (0, 1):
        where = [jax.random.randint(jax.random.fold_in(own_key, axis), (), 0, length) for axis, length in enumerate(drawn.shape)]
        where[longest] = (where[longest] + shift) % drawn.shape[longest]
        spots.append(tuple(where))
    return drawn.at[spots[0]].set(least).at[spots[1]].set(largest)


def level_of(rng, extent, shards, least, top_value):
    def one(axis_at, shards_of):
        steps = jax.random.uniform(jax.random.fold_in(jax.random.fold_in(rng, 6), axis_at), (shards_of,), jnp.float32, least / len(shards), top_value / len(shards))
        return jnp.repeat(jnp.exp(steps), extent[axis_at] // shards_of).reshape((-1,) + (1,) * (len(extent) - axis_at - 1))

    loudness = one(*shards[0])
    for cut in shards[1:]:
        loudness = loudness * one(*cut)
    return loudness


def gaussian(own_key, extent, spread, bound, pieces=(), held_as=jnp.bfloat16):
    drawn = jax.random.normal(own_key, extent, jnp.float32) * spread
    if len(pieces) > 0:
        drawn = level_of(own_key, extent, pieces, -0.22, 0.18) * drawn
    return jnp.clip(drawn, min=-bound, max=bound).astype(held_as)


def setup_inputs(seed: int = 0) -> dict:
    key_list = jax.random.split(jax.random.key(seed), 16)
    return {
        "features": gaussian(key_list[0], (D_IN, NODES), 1.0, 6.0, ((0, 8), (1, 16))),
        "adj_one": gaussian(key_list[1], (N_DOM * PART_TILES, K1, TILE, TILE), (K1 * TILE) ** -0.5, 0.25, ((0, 16),)),
        "src_one": set_ends(jax.random.randint(key_list[2], (N_DOM * PART_TILES, K1), 0, PART_TILES), jax.random.fold_in(key_list[2], 1), 0, PART_TILES - 1).astype(jnp.int32),
        "w_self_one": gaussian(key_list[3], (D_IN, HID), D_IN ** -0.5, 0.21875, ((0, 8),)),
        "w_neigh_one": gaussian(key_list[4], (D_IN, HID), D_IN ** -0.5, 0.21875, ((0, 8),)),
        "bias_one": gaussian(key_list[5], (HID,), 1.0, 4.0, (), jnp.float32),
        "w_self_two": gaussian(key_list[6], (HID, HID), HID ** -0.5, 0.1875),
        "w_neigh_two": gaussian(key_list[7], (HID, HID), HID ** -0.5, 0.1875),
        "bias_two": gaussian(key_list[8], (HID,), 1.0, 4.0, (), jnp.float32),
        "seed_rows": set_ends(jax.random.randint(key_list[9], (N_DOM, N_FEAT, SEEDS_DEV), 0, ROW_DEV), jax.random.fold_in(key_list[9], 1), 0, ROW_DEV - 1).astype(jnp.int32),
        "adj_two": gaussian(key_list[10], (N_DOM, N_FEAT, SEED_T, K2, TILE, TILE), (K2 * TILE) ** -0.5, 0.125, ((0, 16), (1, 8))),
        "src_two": set_ends(jax.random.randint(key_list[11], (N_DOM, N_FEAT, SEED_T, K2), 0, TILE_DEV + 4 * HALO_T), jax.random.fold_in(key_list[11], 1), 0, (TILE_DEV + 4 * HALO_T) - 1).astype(jnp.int32),
        "send_tiles": set_ends(jax.random.randint(key_list[12], (N_DOM, N_FEAT, 4, HALO_T), 0, TILE_DEV), jax.random.fold_in(key_list[12], 1), 0, TILE_DEV - 1).astype(jnp.int32),
        "send_count": draw_send_count(jax.random.fold_in(key_list[15], 71), 0),
        "cotangent": gaussian(key_list[14], (N_DOM, N_FEAT * SEEDS_DEV, HID), 1.0, 6.0, ((0, 16), (1, 8))),
    }


OFFSETS = (-2, -1, 1, 2)


def shift_parts(values, offset):
    filler = jnp.zeros((abs(offset),) + values.shape[1:], values.dtype)
    if offset > 0:
        return jnp.concatenate([filler, values[:-offset]], axis=0)
    return jnp.concatenate([values[-offset:], filler], axis=0)


def reference(features, adj_one, src_one, w_self_one, w_neigh_one, bias_one, w_self_two, w_neigh_two, bias_two, seed_rows, adj_two, src_two, send_tiles, send_count, cotangent):
    slice_width = D_IN // N_FEAT

    def layer_one(part_index):
        columns = lax.dynamic_slice_in_dim(features, part_index * PART_ROWS, PART_ROWS, 1)
        blocks = lax.dynamic_slice_in_dim(adj_one, part_index * PART_TILES, PART_TILES, 0)
        sources = lax.dynamic_slice_in_dim(src_one, part_index * PART_TILES, PART_TILES, 0)
        tiled = columns.reshape(D_IN, PART_TILES, TILE)
        picked = tiled[:, sources]
        gathered = jnp.einsum("ftkj,tkij->fti", picked.astype(jnp.float32), blocks.astype(jnp.float32))
        gathered = gathered.astype(jnp.bfloat16).reshape(D_IN, PART_ROWS)
        own_part = jnp.einsum("sdr,sdh->srh", columns.reshape(N_FEAT, slice_width, PART_ROWS).astype(jnp.float32),
                              w_self_one.reshape(N_FEAT, slice_width, HID).astype(jnp.float32))
        neigh_part = jnp.einsum("sdr,sdh->srh", gathered.reshape(N_FEAT, slice_width, PART_ROWS).astype(jnp.float32),
                                w_neigh_one.reshape(N_FEAT, slice_width, HID).astype(jnp.float32))
        rounded = lax.optimization_barrier((own_part + neigh_part).astype(jnp.bfloat16))
        total = jnp.sum(rounded.astype(jnp.float32), axis=0)
        return jax.nn.relu(total + bias_one).astype(jnp.bfloat16)

    hidden = lax.map(layer_one, jnp.arange(N_DOM, dtype=jnp.int32))
    hidden_tiles = hidden.reshape(N_DOM, N_FEAT, TILE_DEV, TILE, HID)
    outgoing = jax.vmap(jax.vmap(lambda tiles, picks: tiles[picks]))(hidden_tiles, send_tiles)
    live_slots = jnp.arange(HALO_T, dtype=jnp.int32)[None, None, None, :] < send_count[..., None]
    outgoing = jnp.where(live_slots[..., None, None], outgoing, jnp.zeros((), jnp.bfloat16))
    received = [shift_parts(outgoing[:, :, slot_index], OFFSETS[slot_index]) for slot_index in range(4)]
    source_table = jnp.concatenate([hidden_tiles] + received, axis=2)
    device_total = N_DOM * N_FEAT
    table_width = TILE_DEV + 4 * HALO_T

    def layer_two(items):
        table, blocks, sources, chosen_rows, upstream = items
        hidden_rows = table[:TILE_DEV].reshape(ROW_DEV, HID)
        onehot = (sources[:, :, None] == jnp.arange(table_width, dtype=jnp.int32)[None, None, :]).astype(jnp.float32)
        folded = jnp.einsum("sku,skij->siuj", onehot, blocks.astype(jnp.float32))
        folded = folded.astype(jnp.bfloat16).reshape(SEEDS_DEV, table_width * TILE)
        gathered = jnp.dot(folded, table.reshape(table_width * TILE, HID), preferred_element_type=jnp.float32)
        gathered = gathered.astype(jnp.bfloat16)
        chosen = hidden_rows[chosen_rows]
        output = jnp.dot(chosen, w_self_two, preferred_element_type=jnp.float32)
        output = output + jnp.dot(gathered, w_neigh_two, preferred_element_type=jnp.float32) + bias_two
        back_self = jnp.dot(upstream, w_self_two.T, preferred_element_type=jnp.float32)
        back_neigh = jnp.dot(upstream, w_neigh_two.T, preferred_element_type=jnp.float32).astype(jnp.bfloat16)
        table_grad = jnp.dot(folded.T, back_neigh, preferred_element_type=jnp.float32)
        table_grad = table_grad.reshape(table_width, TILE, HID)
        local_grad = table_grad[:TILE_DEV].reshape(ROW_DEV, HID)
        local_grad = local_grad + jnp.zeros((ROW_DEV, HID), jnp.float32).at[chosen_rows].add(back_self)
        return output.astype(jnp.bfloat16), local_grad, table_grad[TILE_DEV:].reshape(4, HALO_T, TILE, HID)

    outputs, local_grads, halo_grads = lax.map(layer_two, (
        source_table.reshape(device_total, table_width, TILE, HID),
        adj_two.reshape(device_total, SEED_T, K2, TILE, TILE),
        src_two.reshape(device_total, SEED_T, K2),
        seed_rows.reshape(device_total, SEEDS_DEV),
        cotangent.reshape(device_total, SEEDS_DEV, HID)))
    halo_grads = halo_grads.reshape(N_DOM, N_FEAT, 4, HALO_T, TILE, HID)
    returned = jnp.stack([shift_parts(halo_grads[:, :, slot_index], -OFFSETS[slot_index]) for slot_index in range(4)], axis=2)
    returned = jnp.where(live_slots[..., None, None], returned, jnp.zeros((), jnp.float32))
    local_tiles = local_grads.reshape(N_DOM, N_FEAT, TILE_DEV, TILE, HID)
    merged = jax.vmap(jax.vmap(lambda grads, picks, extra: grads.at[picks.reshape(-1)].add(extra.reshape(-1, TILE, HID))))(
        local_tiles, send_tiles, returned)
    return outputs.reshape(N_DOM, N_FEAT * SEEDS_DEV, HID), merged.reshape(N_DOM, PART_ROWS, HID)
```

```python
import functools

import jax
import jax.numpy as jnp
from jax import lax
from jax.experimental import pallas as pl
from jax.experimental.pallas import tpu as pltpu
from jax.sharding import PartitionSpec as P

TILE = 128
TILE_DEV = 6
SLOTS = 4
NEAR = 4
MIB = 1 << 20

VMEM = pl.BlockSpec(memory_space=pltpu.VMEM)
SMEM = pl.BlockSpec(memory_space=pltpu.SMEM)


def shifted(shard, by):
    count = lax.axis_size("dom")
    pairs = [(i, i + by) for i in range(count) if 0 <= i + by < count]
    return lax.ppermute(shard, "dom", pairs)


def call(body, outs, in_specs, scratch=(), flops=0, moved=0, **extra):
    return pl.pallas_call(
        body,
        out_shape=outs,
        in_specs=in_specs,
        out_specs=jax.tree.map(lambda _: VMEM, outs),
        scratch_shapes=list(scratch),
        cost_estimate=pl.CostEstimate(flops=flops, bytes_accessed=moved, transcendentals=0),
        compiler_params=pltpu.CompilerParams(vmem_limit_bytes=52 * MIB),
        **extra,
    )


def tn_dot(left, right):
    return lax.dot_general(left, right, (((0,), (0,)), ((), ())), preferred_element_type=jnp.float32)


def nt_dot(left, right):
    return lax.dot_general(left, right, (((1,), (1,)), ((), ())), preferred_element_type=jnp.float32)


def nn_dot(left, right):
    return jnp.dot(left, right, preferred_element_type=jnp.float32)


def order_of(tiles, count):
    listed = []
    for tile in range(TILE_DEV):
        hit = jnp.int32(0)
        for slot in range(SLOTS):
            hit = jnp.where((tiles(slot) == tile) & (slot < count), 1, hit)
        listed.append(hit)
    total = functools.reduce(lambda a, b: a + b, listed)
    places = []
    ahead = jnp.int32(0)
    behind = total
    for tile in range(TILE_DEV):
        places.append(jnp.where(listed[tile] == 1, ahead, behind))
        ahead = ahead + listed[tile]
        behind = behind + (1 - listed[tile])
    return places


def place_of(places, tile):
    at = places[0]
    for other in range(1, TILE_DEV):
        at = jnp.where(tile == other, places[other], at)
    return at


def tile_rows(ref, index):
    return ref.at[pl.ds(pl.multiple_of(index * TILE, TILE), TILE)]


def far_kernel(adj_ref, src_ref, cot_ref, w_ref, back_ref, fold_ref, up_ref, down_ref, acc_ref):
    back = nt_dot(cot_ref[...], w_ref[...]).astype(jnp.bfloat16)
    back_ref[...] = back
    acc_ref[...] = jnp.zeros_like(acc_ref)
    for seed in range(adj_ref.shape[0]):
        rows = pl.ds(seed * TILE, TILE)

        def add(k, _):
            slot = src_ref[seed, k] - TILE_DEV
            low = (slot >= 0) & (slot < SLOTS)
            high = slot >= 3 * SLOTS

            @pl.when(low | high)
            def _():
                at = jnp.where(low, slot, slot - 2 * SLOTS)
                cols = pl.ds(pl.multiple_of(at * TILE, TILE), TILE)
                acc_ref[rows, cols] += adj_ref[seed, k].astype(jnp.float32)

            return 0

        lax.fori_loop(0, adj_ref.shape[1], add, 0, unroll=4)
    fold_ref[...] = acc_ref[...].astype(jnp.bfloat16)
    half = SLOTS * TILE
    up_ref[...] = tn_dot(fold_ref[:, :half], back).astype(jnp.bfloat16).reshape(up_ref.shape)
    down_ref[...] = tn_dot(fold_ref[:, half:], back).astype(jnp.bfloat16).reshape(down_ref.shape)


def near_kernel(
    adj_ref, src_ref, back_ref, meta_ref, fold_ref, own_up_ref, own_down_ref, b_up_ref, b_down_ref, acc_ref, place_ref
):
    acc_ref[...] = jnp.zeros_like(acc_ref)
    for seed in range(adj_ref.shape[0]):
        rows = pl.ds(seed * TILE, TILE)

        def add(k, _):
            slot = src_ref[seed, k]
            local = slot < TILE_DEV
            near = (slot >= TILE_DEV + SLOTS) & (slot < TILE_DEV + 3 * SLOTS)

            @pl.when(local | near)
            def _():
                at = jnp.where(local, slot, slot - SLOTS)
                cols = pl.ds(pl.multiple_of(at * TILE, TILE), TILE)
                acc_ref[rows, cols] += adj_ref[seed, k].astype(jnp.float32)

            return 0

        lax.fori_loop(0, adj_ref.shape[1], add, 0, unroll=4)
    fold_ref[...] = acc_ref[...].astype(jnp.bfloat16)
    back = back_ref[...]
    for far_q, near_q, row, own_ref, b_ref in ((0, 1, 3, own_up_ref, b_up_ref), (3, 2, 1, own_down_ref, b_down_ref)):
        places = order_of(lambda m: meta_ref[row, far_q * SLOTS + m], meta_ref[row, 16 + far_q])
        place_ref[...] = jnp.zeros_like(place_ref)
        for slot in range(SLOTS):
            at = place_of(places, meta_ref[row, near_q * SLOTS + slot])

            @pl.when(slot < meta_ref[row, 16 + near_q])
            def _():
                cols = pl.ds(pl.multiple_of(at * TILE, TILE), TILE)
                start = (TILE_DEV + (near_q - 1) * SLOTS + slot) * TILE
                place_ref[:, cols] += fold_ref[:, start : start + TILE].astype(jnp.float32)

        placed = place_ref[...].astype(jnp.bfloat16)
        own_ref[...] = tn_dot(placed[:, : NEAR * TILE], back).reshape(own_ref.shape)
        b_ref[...] = tn_dot(placed[:, NEAR * TILE :], back).astype(jnp.bfloat16).reshape(b_ref.shape)


def join_kernel(own_up_ref, own_down_ref, far_up_ref, far_down_ref, meta_ref, up_ref, down_ref, sum_ref):
    for far_q, row, own_ref, far_ref, out_ref in (
        (0, 3, own_up_ref, far_up_ref, up_ref),
        (3, 1, own_down_ref, far_down_ref, down_ref),
    ):
        count = meta_ref[row, 16 + far_q]
        places = order_of(lambda m: meta_ref[row, far_q * SLOTS + m], count)
        sum_ref[...] = own_ref[...]
        for slot in range(SLOTS):
            at = jnp.minimum(place_of(places, meta_ref[row, far_q * SLOTS + slot]), NEAR - 1)

            @pl.when(slot < count)
            def _():
                sum_ref[at] += far_ref[slot].astype(jnp.float32)

        out_ref[...] = sum_ref[...].astype(jnp.bfloat16)


def local_kernel(fold_ref, back_ref, cot_ref, w_ref, seeds_ref, out_ref):
    rows = out_ref.shape[0]
    back_self = nt_dot(cot_ref[...], w_ref[...]).astype(jnp.bfloat16)
    hot = lax.broadcasted_iota(jnp.int32, (rows, seeds_ref.shape[1]), 0) == seeds_ref[...]
    hot = hot.astype(jnp.float32).astype(jnp.bfloat16)
    out_ref[...] = nn_dot(hot, back_self) + tn_dot(fold_ref[:, :rows], back_ref[...])


def gather_kernel(src_ref, feat_ref, adj_ref, out_ref):
    step = pl.program_id(0)
    width = feat_ref.shape[0]
    span = out_ref.shape[2]
    out_ref[0, :width] = feat_ref[:, pl.ds(pl.multiple_of(step * span, span), span)]
    for tile in range(adj_ref.shape[0]):
        parts = []
        for k in range(adj_ref.shape[1]):
            source = src_ref[step * adj_ref.shape[0] + tile, k]
            parts.append(feat_ref[:, pl.ds(pl.multiple_of(source * TILE, TILE), TILE)])
        left = jnp.concatenate(parts, axis=1)
        right = jnp.concatenate([adj_ref[tile, k] for k in range(adj_ref.shape[1])], axis=1)
        out_ref[0, width:, tile * TILE : (tile + 1) * TILE] = nt_dot(left, right).astype(jnp.bfloat16)


def hidden_kernel(in_ref, w_ref, bias_ref, meta_ref, hid_ref, a_up_ref, a_down_ref, b_up_ref, b_down_ref):
    depth = in_ref.shape[0] * in_ref.shape[1]
    inputs = in_ref[...].reshape(depth, in_ref.shape[2])
    weights = w_ref[...].reshape(depth, w_ref.shape[2])
    total = tn_dot(inputs, weights) + bias_ref[...]
    hidden = jnp.maximum(total, 0.0).astype(jnp.bfloat16)
    hid_ref[...] = hidden.reshape(hid_ref.shape)
    for far_q, a_ref, b_ref in ((3, a_up_ref, b_up_ref), (0, a_down_ref, b_down_ref)):
        places = order_of(lambda m: meta_ref[2, far_q * SLOTS + m], meta_ref[2, 16 + far_q])
        for tile in range(TILE_DEV):

            @pl.when(places[tile] < NEAR)
            def _():
                a_ref[jnp.minimum(places[tile], NEAR - 1)] = hid_ref[tile]

            @pl.when(places[tile] >= NEAR)
            def _():
                b_ref[jnp.maximum(places[tile] - NEAR, 0)] = hid_ref[tile]


def mid_kernel(
    fold_ref, hid_ref, a_up_ref, b_up_ref, a_down_ref, b_down_ref, meta_ref, seeds_ref, w_ref, bias_ref,
    part_ref, self_ref, table_ref,
):
    rows = TILE_DEV * TILE
    table_ref[:rows] = hid_ref[...].reshape(rows, hid_ref.shape[2])
    start = TILE_DEV
    for near_q, far_q, row, a_ref, b_ref in ((1, 0, 3, a_down_ref, b_down_ref), (2, 3, 1, a_up_ref, b_up_ref)):
        places = order_of(lambda m: meta_ref[row, far_q * SLOTS + m], meta_ref[row, 16 + far_q])
        for slot in range(SLOTS):
            at = place_of(places, meta_ref[row, near_q * SLOTS + slot])
            live = slot < meta_ref[row, 16 + near_q]
            to = slice((start + slot) * TILE, (start + slot + 1) * TILE)

            @pl.when(live & (at < NEAR))
            def _():
                table_ref[to] = a_ref[jnp.minimum(at, NEAR - 1)]

            @pl.when(live & (at >= NEAR))
            def _():
                table_ref[to] = b_ref[jnp.maximum(at - NEAR, 0)]

            @pl.when(jnp.logical_not(live))
            def _():
                table_ref[to] = jnp.zeros((TILE, table_ref.shape[1]), table_ref.dtype)

        start += SLOTS
    part_ref[...] = nn_dot(fold_ref[...], table_ref[...])
    hot = lax.broadcasted_iota(jnp.int32, (rows, seeds_ref.shape[1]), 0) == seeds_ref[...]
    hot = hot.astype(jnp.float32).astype(jnp.bfloat16)
    chosen = tn_dot(hot, table_ref[:rows]).astype(jnp.bfloat16)
    self_ref[...] = nn_dot(chosen, w_ref[...]) + bias_ref[...]


def last_kernel(fold_ref, f_up_ref, f_down_ref, meta_ref, part_ref, self_ref, w_ref, out_ref, table_ref):
    start = 0
    for far_q, row, f_ref in ((0, 4, f_down_ref), (3, 0, f_up_ref)):
        count = meta_ref[row, 16 + far_q]
        places = order_of(lambda m: meta_ref[row, far_q * SLOTS + m], count)
        for slot in range(SLOTS):
            at = place_of(places, meta_ref[row, far_q * SLOTS + slot])
            to = slice((start + slot) * TILE, (start + slot + 1) * TILE)

            @pl.when(slot < count)
            def _():
                table_ref[to] = f_ref[jnp.minimum(at, NEAR - 1)]

            @pl.when(slot >= count)
            def _():
                table_ref[to] = jnp.zeros((TILE, table_ref.shape[1]), table_ref.dtype)

        start += SLOTS
    gathered = (part_ref[...] + nn_dot(fold_ref[...], table_ref[...])).astype(jnp.bfloat16)
    out_ref[...] = (self_ref[...] + nn_dot(gathered, w_ref[...])).astype(jnp.bfloat16)


def merge_kernel(local_ref, a_up_ref, b_up_ref, a_down_ref, b_down_ref, meta_ref, out_ref):
    up = order_of(lambda m: meta_ref[2, 3 * SLOTS + m], meta_ref[2, 16 + 3])
    down = order_of(lambda m: meta_ref[2, m], meta_ref[2, 16])
    for tile in range(TILE_DEV):
        to = slice(tile * TILE, (tile + 1) * TILE)
        out_ref[to] = local_ref[to]
        for places, a_ref, b_ref in ((up, a_up_ref, b_up_ref), (down, a_down_ref, b_down_ref)):

            @pl.when(places[tile] < NEAR)
            def _():
                out_ref[to] += a_ref[jnp.minimum(places[tile], NEAR - 1)].astype(jnp.float32)

            @pl.when(places[tile] >= NEAR)
            def _():
                out_ref[to] += b_ref[jnp.maximum(places[tile] - NEAR, 0)].astype(jnp.float32)


def shards(
    features,
    adj_one,
    src_one,
    w_self_one,
    w_neigh_one,
    bias_one,
    w_self_two,
    w_neigh_two,
    bias_two,
    seed_rows,
    adj_two,
    src_two,
    send_tiles,
    send_count,
    cotangent,
):
    bf16, f32 = jnp.bfloat16, jnp.float32
    width = features.shape[0]
    part_tiles = adj_one.shape[0]
    hid = w_self_two.shape[0]
    feat_count = lax.axis_size("feat")
    row_dev = features.shape[1] // feat_count
    seeds = cotangent.shape[1]
    blocks, sources = adj_two[0, 0], src_two[0, 0]
    upstream = cotangent[0]
    shape = jax.ShapeDtypeStruct

    own = jnp.concatenate([send_tiles.reshape(-1), send_count.reshape(-1), jnp.zeros((4,), jnp.int32)])
    lists = lax.all_gather(own, "dom")
    lists = jnp.pad(lists, ((2, 2), (0, 0)))
    meta = lax.dynamic_slice_in_dim(lists, lax.axis_index("dom"), 5, 0)
    weights = lax.all_gather(jnp.concatenate([w_self_one, w_neigh_one]), "feat")

    quad = shape((NEAR, TILE, hid), bf16)
    pair = shape((TILE_DEV - NEAR, TILE, hid), bf16)
    quad32 = shape((NEAR, TILE, hid), f32)
    far_cols, near_cols = 2 * SLOTS * TILE, (TILE_DEV + 2 * SLOTS) * TILE

    back, fold_far, far_up, far_down = call(
        far_kernel,
        (shape((seeds, hid), bf16), shape((seeds, far_cols), bf16), quad, quad),
        [VMEM, SMEM, VMEM, VMEM],
        [pltpu.VMEM((seeds, far_cols), f32)],
        flops=4 * seeds * hid * hid,
        moved=8 * MIB,
    )(blocks, sources, upstream, w_neigh_two)
    got_far_up = shifted(far_up, 1)
    got_far_down = shifted(far_down, -1)

    sent = pl.pallas_call(
        gather_kernel,
        grid=(feat_count,),
        in_specs=[
            SMEM,
            pl.BlockSpec((width, features.shape[1]), lambda i: (0, 0)),
            pl.BlockSpec((part_tiles // feat_count,) + adj_one.shape[1:], lambda i: (i, 0, 0, 0)),
        ],
        out_specs=pl.BlockSpec((1, 2 * width, row_dev), lambda i: (i, 0, 0)),
        out_shape=shape((feat_count, 2 * width, row_dev), bf16),
        cost_estimate=pl.CostEstimate(flops=1200 * MIB, bytes_accessed=10 * MIB, transcendentals=0),
        compiler_params=pltpu.CompilerParams(vmem_limit_bytes=32 * MIB),
    )(src_one, features, adj_one)

    fold_near, own_up, own_down, b_up, b_down = call(
        near_kernel,
        (shape((seeds, near_cols), bf16), quad32, quad32, pair, pair),
        [VMEM, SMEM, VMEM, SMEM],
        [pltpu.VMEM((seeds, near_cols), f32), pltpu.VMEM((seeds, TILE_DEV * TILE), f32)],
        flops=3 * seeds * hid * hid,
        moved=12 * MIB,
    )(blocks, sources, back, meta)
    got_b_up = shifted(b_up, 1)
    got_b_down = shifted(b_down, -1)

    taken = lax.all_to_all(sent, "feat", 0, 0)

    a_up, a_down = call(
        join_kernel,
        (quad, quad),
        [VMEM, VMEM, VMEM, VMEM, SMEM],
        [pltpu.VMEM(quad32.shape, f32)],
        moved=8 * MIB,
    )(own_up, own_down, got_far_up, got_far_down, meta)
    got_a_up = shifted(a_up, 1)
    got_a_down = shifted(a_down, -1)

    hidden, h_up, h_down, i_up, i_down = call(
        hidden_kernel,
        (shape((TILE_DEV, TILE, hid), bf16), quad, quad, pair, pair),
        [VMEM, VMEM, VMEM, SMEM],
        flops=2 * row_dev * 2 * width * feat_count * hid,
        moved=10 * MIB,
    )(taken, weights, bias_one[None], meta)
    got_h_up = shifted(h_up, 1)
    got_h_down = shifted(h_down, -1)
    got_i_up = shifted(i_up, 1)
    got_i_down = shifted(i_down, -1)
    next_up = shifted(got_h_up, 1)
    next_down = shifted(got_h_down, -1)

    local = call(
        local_kernel,
        shape((row_dev, hid), f32),
        [VMEM] * 5,
        flops=5 * seeds * hid * hid,
        moved=8 * MIB,
    )(fold_near, back, upstream, w_self_two, seed_rows[0])

    part, self_term = call(
        mid_kernel,
        (shape((seeds, hid), f32), shape((seeds, hid), f32)),
        [VMEM] * 6 + [SMEM] + [VMEM] * 3,
        [pltpu.VMEM((near_cols, hid), bf16)],
        flops=7 * seeds * hid * hid,
        moved=16 * MIB,
    )(fold_near, hidden, got_h_up, got_i_up, got_h_down, got_i_down, meta, seed_rows[0], w_self_two, bias_two[None])
    layer_out = call(
        last_kernel,
        shape((seeds, hid), bf16),
        [VMEM] * 3 + [SMEM] + [VMEM] * 3,
        [pltpu.VMEM((far_cols, hid), bf16)],
        flops=4 * seeds * hid * hid,
        moved=10 * MIB,
    )(fold_far, next_up, next_down, meta, part, self_term, w_neigh_two)
    grads = call(
        merge_kernel, shape((row_dev, hid), f32), [VMEM] * 5 + [SMEM], moved=9 * MIB
    )(local, got_a_down, got_b_down, got_a_up, got_b_up, meta)
    return (layer_out[None], grads[None])


def solution(mesh):
    return jax.shard_map(
        shards,
        mesh=mesh,
        in_specs=(
            P("feat", "dom"),
            P("dom", None, None, None),
            P("dom", None),
            P("feat", None),
            P("feat", None),
            P(),
            P(),
            P(),
            P(),
            P("dom", "feat", None),
            P("dom", "feat", None, None, None, None),
            P("dom", "feat", None, None),
            P("dom", "feat", None, None),
            P("dom", "feat", None),
            P("dom", "feat", None),
        ),
        out_specs=(P("dom", "feat", None), P("dom", "feat", None)),
        check_vma=False,
    )
```

```python
import functools

import jax
import jax.numpy as jnp
from jax import lax
from jax.experimental import pallas as pl
from jax.experimental.pallas import tpu as pltpu
from jax.sharding import PartitionSpec as P

TILE = 128
TILE_DEV = 6
SLOTS = 4
NEAR = 4
ROWS = 8
MIB = 1 << 20
OFFSETS = (-2, -1, 1, 2)
GIGA = 1 << 30

VMEM = pl.BlockSpec(memory_space=pltpu.VMEM)
SMEM = pl.BlockSpec(memory_space=pltpu.SMEM)
ANY = pl.BlockSpec(memory_space=pl.ANY)


def shifted(shard, by):
    count = lax.axis_size("dom")
    return lax.ppermute(shard, "dom", [(i, (i + by) % count) for i in range(count)])


def call(body, outs, in_specs, scratch=(), cost=1, vmem=32):
    return pl.pallas_call(
        body,
        out_shape=outs,
        in_specs=in_specs,
        out_specs=jax.tree.map(lambda _: VMEM, outs),
        scratch_shapes=list(scratch),
        cost_estimate=pl.CostEstimate(flops=cost * GIGA, bytes_accessed=1, transcendentals=0),
        compiler_params=pltpu.CompilerParams(vmem_limit_bytes=vmem * MIB),
    )


def tn_dot(left, right):
    return lax.dot_general(left, right, (((0,), (0,)), ((), ())), preferred_element_type=jnp.float32)


def nt_dot(left, right):
    return lax.dot_general(left, right, (((1,), (1,)), ((), ())), preferred_element_type=jnp.float32)


def nn_dot(left, right):
    return jnp.dot(left, right, preferred_element_type=jnp.float32)


def order_of(tiles, count):
    listed = []
    for tile in range(TILE_DEV):
        hit = jnp.int32(0)
        for slot in range(SLOTS):
            hit = jnp.where((tiles(slot) == tile) & (slot < count), 1, hit)
        listed.append(hit)
    total = functools.reduce(lambda a, b: a + b, listed)
    places = []
    ahead = jnp.int32(0)
    behind = total
    for tile in range(TILE_DEV):
        places.append(jnp.where(listed[tile] == 1, ahead, behind))
        ahead = ahead + listed[tile]
        behind = behind + (1 - listed[tile])
    return places


def place_of(places, tile):
    at = places[0]
    for other in range(1, TILE_DEV):
        at = jnp.where(tile == other, places[other], at)
    return at


def halves_kernel(self_ref, neigh_ref, out_ref, sems):
    copies = [
        pltpu.make_async_copy((self_ref, neigh_ref)[i % 2], out_ref.at[i], sems.at[i]) for i in range(out_ref.shape[0])
    ]
    for copy in copies:
        copy.start()
    for copy in copies:
        copy.wait()


def far_kernel(
    adj_ref, src_ref, cot_ref, w_ref, after_ref,
    back_ref, fold_ref, up_ref, down_ref, adj_buf, cot_buf, w_buf, acc_ref, sems,
):
    seeds = adj_ref.shape[0]
    loads = [pltpu.make_async_copy(adj_ref.at[s], adj_buf.at[s], sems.at[s]) for s in range(seeds)]
    load_w = pltpu.make_async_copy(w_ref, w_buf, sems.at[seeds])
    load_cot = pltpu.make_async_copy(cot_ref, cot_buf, sems.at[seeds + 1])
    for load in loads:
        load.start()
    load_cot.start()
    load_w.start()
    acc_ref[...] = jnp.zeros_like(acc_ref)
    for seed in range(seeds):
        loads[seed].wait()
        rows = pl.ds(seed * TILE, TILE)

        def add(k, _):
            slot = src_ref[seed, k] - TILE_DEV
            low = (slot >= 0) & (slot < SLOTS)
            high = slot >= 3 * SLOTS

            @pl.when(low | high)
            def _():
                at = jnp.where(low, slot, slot - 2 * SLOTS)
                cols = pl.ds(pl.multiple_of(at * TILE, TILE), TILE)
                acc_ref[rows, cols] += adj_buf[seed, k].astype(jnp.float32)

            return 0

        lax.fori_loop(0, adj_ref.shape[1], add, 0, unroll=4)
    fold_ref[...] = acc_ref[...].astype(jnp.bfloat16)
    load_cot.wait()
    load_w.wait()
    back = nt_dot(cot_buf[...], w_buf[...]).astype(jnp.bfloat16)
    back_ref[...] = back
    half = SLOTS * TILE
    up_ref[...] = tn_dot(fold_ref[:, :half], back).astype(jnp.bfloat16).reshape(up_ref.shape)
    down_ref[...] = tn_dot(fold_ref[:, half:], back).astype(jnp.bfloat16).reshape(down_ref.shape)


def near_kernel(adj_ref, src_ref, back_ref, after_ref, fold_ref, up_ref, down_ref, acc_ref):
    acc_ref[...] = jnp.zeros_like(acc_ref)
    for seed in range(adj_ref.shape[0]):
        rows = pl.ds(seed * TILE, TILE)

        def add(k, _):
            slot = src_ref[seed, k]
            local = slot < TILE_DEV
            near = (slot >= TILE_DEV + SLOTS) & (slot < TILE_DEV + 3 * SLOTS)

            @pl.when(local | near)
            def _():
                at = jnp.where(local, slot, slot - SLOTS)
                cols = pl.ds(pl.multiple_of(at * TILE, TILE), TILE)
                acc_ref[rows, cols] += adj_ref[seed, k].astype(jnp.float32)

            return 0

        lax.fori_loop(0, adj_ref.shape[1], add, 0, unroll=4)
    fold_ref[...] = acc_ref[...].astype(jnp.bfloat16)
    back = back_ref[...]
    start, half = TILE_DEV * TILE, SLOTS * TILE
    up_ref[...] = tn_dot(fold_ref[:, start : start + half], back).astype(jnp.bfloat16).reshape(up_ref.shape)
    down_ref[...] = tn_dot(fold_ref[:, start + half :], back).astype(jnp.bfloat16).reshape(down_ref.shape)


def local_kernel(fold_ref, back_ref, cot_ref, w_ref, seeds_ref, after_up_ref, after_down_ref, out_ref):
    rows = out_ref.shape[0]
    back_self = nt_dot(cot_ref[...], w_ref[...]).astype(jnp.bfloat16)
    hot = lax.broadcasted_iota(jnp.int32, (rows, seeds_ref.shape[1]), 0) == seeds_ref[...]
    hot = hot.astype(jnp.float32).astype(jnp.bfloat16)
    out_ref[...] = nn_dot(hot, back_self) + tn_dot(fold_ref[:, :rows], back_ref[...])


def gather_kernel(src_ref, feat_ref, adj_ref, after_ref, out_ref):
    step = pl.program_id(0)
    width = feat_ref.shape[0]
    span = out_ref.shape[2]
    out_ref[0, :width] = feat_ref[:, pl.ds(pl.multiple_of(step * span, span), span)]
    for tile in range(adj_ref.shape[0]):
        parts = []
        for k in range(adj_ref.shape[1]):
            source = src_ref[k, step * adj_ref.shape[0] + tile]
            parts.append(feat_ref[:, pl.ds(pl.multiple_of(source * TILE, TILE), TILE)])
        left = jnp.concatenate(parts, axis=1)
        right = jnp.concatenate([adj_ref[tile, k] for k in range(adj_ref.shape[1])], axis=1)
        out_ref[0, width:, tile * TILE : (tile + 1) * TILE] = nt_dot(left, right).astype(jnp.bfloat16)


def hidden_kernel(
    in_ref, mine_ref, other_ref, bias_ref, odd_ref, tiles_ref, count_ref, after_ref,
    hid_ref, up_ref, down_ref, turned_ref, w_ref,
):
    slices, width, span = in_ref.shape[0], in_ref.shape[1] // 2, in_ref.shape[2]
    depth = slices * width

    @pl.when(pl.program_id(0) == 0)
    def _():
        turned_ref[:, :depth] = in_ref[:, :width].reshape(depth, span).T
        turned_ref[:, depth:] = in_ref[:, width:].reshape(depth, span).T

    w_ref[pl.ds(pl.multiple_of(odd_ref[0] * depth, depth), depth)] = mine_ref[...]
    w_ref[pl.ds(pl.multiple_of((1 - odd_ref[0]) * depth, depth), depth)] = other_ref[...]
    total = nn_dot(turned_ref[...], w_ref[...])
    hidden = jnp.maximum(total + bias_ref[...], 0.0).astype(jnp.bfloat16)
    hid_ref[...] = hidden.reshape(hid_ref.shape)
    shape = (2 * ROWS, up_ref.shape[1])
    row = lax.broadcasted_iota(jnp.int32, shape, 0)
    block = (lax.broadcasted_iota(jnp.int32, shape, 1) + pl.program_id(0) * shape[1]) // TILE
    for near_q, far_q, out_ref in ((2, 3, up_ref), (1, 0, down_ref)):
        places = order_of(lambda m: tiles_ref[far_q, m], count_ref[far_q])
        for tile in range(TILE_DEV):

            @pl.when(places[tile] < NEAR)
            def _():
                at = jnp.minimum(places[tile], NEAR - 1) * TILE
                out_ref[pl.ds(pl.multiple_of(at, TILE), TILE)] = hid_ref[tile]

        marks = jnp.zeros(shape, jnp.float32)
        for first, q in ((0, near_q), (SLOTS, far_q)):
            for slot in range(SLOTS):
                at = jnp.where(slot < count_ref[q], place_of(places, tiles_ref[q, slot]), -1)
                marks = jnp.where((row == first + slot) & (block == at), 1.0, marks)
        out_ref[NEAR * TILE :] = marks.astype(jnp.bfloat16)


def merge_kernel(
    local_ref, from_0_ref, from_1_ref, from_2_ref, from_3_ref, hid_ref, tiles_ref, count_ref,
    out_ref, rest_up_ref, rest_down_ref,
):
    out_ref[...] = local_ref[...]
    for q, ref in enumerate((from_0_ref, from_1_ref, from_2_ref, from_3_ref)):
        for slot in range(SLOTS):

            @pl.when(slot < count_ref[q])
            def _():
                at = pl.multiple_of(tiles_ref[q, slot] * TILE, TILE)
                out_ref[pl.ds(at, TILE)] += ref[slot].astype(jnp.float32)

    for far_q, rest_ref in ((3, rest_up_ref), (0, rest_down_ref)):
        places = order_of(lambda m: tiles_ref[far_q, m], count_ref[far_q])
        for tile in range(TILE_DEV):

            @pl.when(places[tile] >= NEAR)
            def _():
                rest_ref[jnp.maximum(places[tile] - NEAR, 0)] = hid_ref[tile]


def placed(fold_ref, start, mark_ref, first, count, out_ref, to):
    marks = mark_ref[NEAR * TILE :].astype(jnp.float32)
    blocks = [
        fold_ref[:, (start + slot) * TILE : (start + slot + 1) * TILE].astype(jnp.float32) for slot in range(SLOTS)
    ]
    for place in range(count):
        cols = slice(place * TILE, (place + 1) * TILE)
        total = sum(blocks[slot] * marks[first + slot : first + slot + 1, cols] for slot in range(SLOTS))
        out_ref[:, (to + place) * TILE : (to + place + 1) * TILE] = total.astype(jnp.bfloat16)


def mid_kernel(
    fold_ref, hid_ref, a_up_ref, rest_up_ref, a_down_ref, rest_down_ref, seeds_ref, w_ref, bias_ref,
    part_ref, self_ref, placed_ref, table_ref,
):
    rows = TILE_DEV * TILE
    quad = NEAR * TILE
    pair = rows - quad
    hidden = hid_ref[...].reshape(rows, hid_ref.shape[2])
    start = 0
    for first, a_ref, rest_ref in ((TILE_DEV, a_down_ref, rest_down_ref), (TILE_DEV + SLOTS, a_up_ref, rest_up_ref)):
        placed(fold_ref, first, a_ref, 0, TILE_DEV, placed_ref, start // TILE)
        table_ref[start : start + quad] = a_ref[:quad]
        table_ref[start + quad : start + rows] = rest_ref[...].reshape(pair, rest_ref.shape[2])
        start += rows
    part_ref[...] = nn_dot(fold_ref[:, :rows], hidden) + nn_dot(placed_ref[...], table_ref[...])
    hot = lax.broadcasted_iota(jnp.int32, (rows, seeds_ref.shape[1]), 0) == seeds_ref[...]
    hot = hot.astype(jnp.float32).astype(jnp.bfloat16)
    chosen = tn_dot(hot, hidden).astype(jnp.bfloat16)
    self_ref[...] = nn_dot(chosen, w_ref[...]) + bias_ref[...]


def last_kernel(fold_ref, f_up_ref, f_down_ref, part_ref, self_ref, w_ref, out_ref, placed_ref):
    quad = NEAR * TILE
    placed(fold_ref, 0, f_down_ref, SLOTS, NEAR, placed_ref, 0)
    placed(fold_ref, SLOTS, f_up_ref, SLOTS, NEAR, placed_ref, NEAR)
    gathered = part_ref[...] + nn_dot(placed_ref[:, :quad], f_down_ref[:quad])
    gathered = (gathered + nn_dot(placed_ref[:, quad:], f_up_ref[:quad])).astype(jnp.bfloat16)
    out_ref[...] = (self_ref[...] + nn_dot(gathered, w_ref[...])).astype(jnp.bfloat16)


def shards(
    features,
    adj_one,
    src_one,
    w_self_one,
    w_neigh_one,
    bias_one,
    w_self_two,
    w_neigh_two,
    bias_two,
    seed_rows,
    adj_two,
    src_two,
    send_tiles,
    send_count,
    cotangent,
):
    bf16, f32 = jnp.bfloat16, jnp.float32
    width = features.shape[0]
    part_tiles = adj_one.shape[0]
    hid = w_self_two.shape[0]
    feat_count = lax.axis_size("feat")
    row_dev = features.shape[1] // feat_count
    seeds = cotangent.shape[1]
    blocks, sources = adj_two[0, 0], src_two[0, 0]
    upstream = cotangent[0]
    shape = jax.ShapeDtypeStruct

    lists = send_tiles[0, 0]
    partner = lax.axis_index("dom") + jnp.array(OFFSETS, jnp.int32)
    inside = (partner >= 0) & (partner < lax.axis_size("dom"))
    counts = jnp.where(inside, send_count[0, 0], 0)
    quad = shape((NEAR, TILE, hid), bf16)
    pair = shape((TILE_DEV - NEAR, TILE, hid), bf16)
    quad_marked = shape((NEAR * TILE + 2 * ROWS, hid), bf16)
    far_cols, near_cols = 2 * SLOTS * TILE, (TILE_DEV + 2 * SLOTS) * TILE

    halves = call(
        halves_kernel,
        shape((feat_count, width, hid), bf16),
        [ANY, ANY],
        [pltpu.SemaphoreType.DMA((feat_count,))],
        vmem=56,
    )(w_self_one, w_neigh_one)
    back, fold_far, far_up, far_down = call(
        far_kernel,
        (shape((seeds, hid), bf16), shape((seeds, far_cols), bf16), quad, quad),
        [ANY, SMEM, ANY, ANY, ANY],
        [
            pltpu.VMEM(blocks.shape, bf16),
            pltpu.VMEM((seeds, hid), bf16),
            pltpu.VMEM((hid, hid), bf16),
            pltpu.VMEM((seeds, far_cols), f32),
            pltpu.SemaphoreType.DMA((blocks.shape[0] + 2,)),
        ],
        vmem=56,
            )(blocks, sources, upstream, w_neigh_two, halves)
    got_far_up = shifted(far_up, 1)
    got_far_down = shifted(far_down, -1)

    sent = pl.pallas_call(
        gather_kernel,
        grid=(feat_count,),
        in_specs=[
            SMEM,
            pl.BlockSpec((width, features.shape[1]), lambda i: (0, 0)),
            pl.BlockSpec((part_tiles // feat_count,) + adj_one.shape[1:], lambda i: (i, 0, 0, 0)),
            ANY,
        ],
        out_specs=pl.BlockSpec((1, 2 * width, row_dev), lambda i: (i, 0, 0)),
        out_shape=shape((feat_count, 2 * width, row_dev), bf16),
        cost_estimate=pl.CostEstimate(flops=100 * GIGA, bytes_accessed=1, transcendentals=0),
        compiler_params=pltpu.CompilerParams(vmem_limit_bytes=56 * MIB),
    )(src_one.T, features, adj_one, back)
    taken = lax.all_to_all(sent, "feat", 0, 0)
    halves = lax.all_to_all(halves, "feat", 0, 0)
    halves = halves.reshape(feat_count * width, hid)
    swapped = lax.ppermute(halves, "feat", [(i, i ^ 1) for i in range(feat_count)])
    odd = (lax.axis_index("feat") % 2).astype(jnp.int32)[None]

    fold_near, near_up, near_down = call(
        near_kernel,
        (shape((seeds, near_cols), bf16), quad, quad),
        [VMEM, SMEM, VMEM, ANY],
        [pltpu.VMEM((seeds, near_cols), f32)],
        vmem=24,
    )(blocks, sources, back, sent)
    grad_1 = shifted(near_up, 1)
    grad_2 = shifted(near_down, -1)
    grad_0 = shifted(got_far_up, 1)
    grad_3 = shifted(got_far_down, -1)

    local = call(
        local_kernel,
        shape((row_dev, hid), f32),
        [VMEM] * 5 + [ANY] * 2,
        cost=20,
        vmem=28,
    )(fold_near, back, upstream, w_self_two, seed_rows[0], got_far_up, got_far_down)

    chunk = hid // 4
    hidden, h_up, h_down = pl.pallas_call(
        hidden_kernel,
        grid=(hid // chunk,),
        in_specs=[
            pl.BlockSpec(taken.shape, lambda j: (0, 0, 0)),
            pl.BlockSpec((feat_count * width, chunk), lambda j: (0, j)),
            pl.BlockSpec((feat_count * width, chunk), lambda j: (0, j)),
            pl.BlockSpec((1, chunk), lambda j: (0, j)),
            SMEM,
            SMEM,
            SMEM,
            ANY,
        ],
        out_specs=[
            pl.BlockSpec((TILE_DEV, TILE, chunk), lambda j: (0, 0, j)),
            pl.BlockSpec((quad_marked.shape[0], chunk), lambda j: (0, j)),
            pl.BlockSpec((quad_marked.shape[0], chunk), lambda j: (0, j)),
        ],
        out_shape=(shape((TILE_DEV, TILE, hid), bf16), quad_marked, quad_marked),
        scratch_shapes=[
            pltpu.VMEM((row_dev, 2 * width * feat_count), bf16),
            pltpu.VMEM((2 * width * feat_count, chunk), bf16),
        ],
        cost_estimate=pl.CostEstimate(flops=GIGA, bytes_accessed=1, transcendentals=0),
        compiler_params=pltpu.CompilerParams(vmem_limit_bytes=24 * MIB),
    )(taken, halves, swapped, bias_one[None], odd, lists, counts, local)
    got_h_up = shifted(h_up, 1)
    got_h_down = shifted(h_down, -1)
    next_up = shifted(got_h_up, 1)
    next_down = shifted(got_h_down, -1)
    grads, rest_up, rest_down = call(
        merge_kernel, (shape((row_dev, hid), f32), pair, pair), [VMEM] * 6 + [SMEM] * 2, vmem=24
    )(local, grad_0, grad_1, grad_2, grad_3, hidden, lists, counts)
    got_rest_up = shifted(rest_up, 1)
    got_rest_down = shifted(rest_down, -1)

    part, self_term = call(
        mid_kernel,
        (shape((seeds, hid), f32), shape((seeds, hid), f32)),
        [VMEM] * 9,
        [pltpu.VMEM((seeds, 2 * row_dev), bf16), pltpu.VMEM((2 * row_dev, hid), bf16)],
        cost=100,
        vmem=32,
    )(
        fold_near, hidden, got_h_up, got_rest_up, got_h_down, got_rest_down,
        seed_rows[0], w_self_two, bias_two[None],
    )
    layer_out = call(
        last_kernel,
        shape((seeds, hid), bf16),
        [VMEM] * 6,
        [pltpu.VMEM((seeds, far_cols), bf16)],
        vmem=20,
    )(fold_far, next_up, next_down, part, self_term, w_neigh_two)
    return (layer_out[None], grads[None])


def solution(mesh):
    return jax.shard_map(
        shards,
        mesh=mesh,
        in_specs=(
            P("feat", "dom"),
            P("dom", None, None, None),
            P("dom", None),
            P("feat", None),
            P("feat", None),
            P(),
            P(),
            P(),
            P(),
            P("dom", "feat", None),
            P("dom", "feat", None, None, None, None),
            P("dom", "feat", None, None),
            P("dom", "feat", None, None),
            P("dom", "feat", None),
            P("dom", "feat", None),
        ),
        out_specs=(P("dom", "feat", None), P("dom", "feat", None)),
        check_vma=False,
    )
```

```python
import functools

import jax
import jax.numpy as jnp
from jax import lax
from jax.experimental import pallas as pl
from jax.experimental.pallas import tpu as pltpu
from jax.sharding import PartitionSpec as P

TILE = 128
TILE_DEV = 6
SLOTS = 4
NEAR = 4
ROWS = 8
MIB = 1 << 20
OFFSETS = (-2, -1, 1, 2)
GIGA = 1 << 30

VMEM = pl.BlockSpec(memory_space=pltpu.VMEM)
SMEM = pl.BlockSpec(memory_space=pltpu.SMEM)
ANY = pl.BlockSpec(memory_space=pl.ANY)


def open_shift(shard, by):
    count = lax.axis_size("dom")
    return lax.ppermute(shard, "dom", [(i, i + by) for i in range(count) if 0 <= i + by < count])


def shifted(shard, by):
    count = lax.axis_size("dom")
    return lax.ppermute(shard, "dom", [(i, (i + by) % count) for i in range(count)])


def call(body, outs, in_specs, scratch=(), cost=1, vmem=32, out_specs=None):
    return pl.pallas_call(
        body,
        out_shape=outs,
        in_specs=in_specs,
        out_specs=out_specs or jax.tree.map(lambda _: VMEM, outs),
        scratch_shapes=list(scratch),
        cost_estimate=pl.CostEstimate(flops=cost * GIGA, bytes_accessed=1, transcendentals=0),
        compiler_params=pltpu.CompilerParams(vmem_limit_bytes=vmem * MIB),
    )


def tn_dot(left, right):
    return lax.dot_general(left, right, (((0,), (0,)), ((), ())), preferred_element_type=jnp.float32)


def nt_dot(left, right):
    return lax.dot_general(left, right, (((1,), (1,)), ((), ())), preferred_element_type=jnp.float32)


def nn_dot(left, right):
    return jnp.dot(left, right, preferred_element_type=jnp.float32)


def order_of(tiles, count):
    listed = []
    for tile in range(TILE_DEV):
        hit = jnp.int32(0)
        for slot in range(SLOTS):
            hit = jnp.where((tiles(slot) == tile) & (slot < count), 1, hit)
        listed.append(hit)
    total = functools.reduce(lambda a, b: a + b, listed)
    places = []
    ahead = jnp.int32(0)
    behind = total
    for tile in range(TILE_DEV):
        places.append(jnp.where(listed[tile] == 1, ahead, behind))
        ahead = ahead + listed[tile]
        behind = behind + (1 - listed[tile])
    return places


def place_of(places, tile):
    at = places[0]
    for other in range(1, TILE_DEV):
        at = jnp.where(tile == other, places[other], at)
    return at


def halves_kernel(self_ref, neigh_ref, after_ref, out_ref, buf, sems):
    loads = [pltpu.make_async_copy(ref, buf.at[i], sems.at[i]) for i, ref in enumerate((self_ref, neigh_ref))]
    stores = [pltpu.make_async_copy(buf.at[i % 2], out_ref.at[i], sems.at[2 + i]) for i in range(out_ref.shape[0])]
    for load in loads:
        load.start()
    for kind, load in enumerate(loads):
        load.wait()
        for store in stores[kind::2]:
            store.start()
    for store in stores:
        store.wait()


def far_kernel(
    adj_ref, src_ref, cot_ref, w_ref,
    back_ref, fold_ref, up_ref, down_ref, adj_buf, cot_buf, w_buf, acc_ref, sems,
):
    seeds = adj_ref.shape[0]
    loads = [pltpu.make_async_copy(adj_ref.at[s], adj_buf.at[s], sems.at[s]) for s in range(seeds)]
    load_w = pltpu.make_async_copy(w_ref, w_buf, sems.at[seeds])
    load_cot = pltpu.make_async_copy(cot_ref, cot_buf, sems.at[seeds + 1])
    for load in loads:
        load.start()
    load_cot.start()
    load_w.start()
    acc_ref[...] = jnp.zeros_like(acc_ref)
    for seed in range(seeds):
        loads[seed].wait()
        rows = pl.ds(seed * TILE, TILE)

        def add(k, _):
            slot = src_ref[seed, k] - TILE_DEV
            low = (slot >= 0) & (slot < SLOTS)
            high = slot >= 3 * SLOTS

            @pl.when(low | high)
            def _():
                at = jnp.where(low, slot, slot - 2 * SLOTS)
                cols = pl.ds(pl.multiple_of(at * TILE, TILE), TILE)
                acc_ref[rows, cols] += adj_buf[seed, k].astype(jnp.float32)

            return 0

        lax.fori_loop(0, adj_ref.shape[1], add, 0, unroll=4)
    fold_ref[...] = acc_ref[...].astype(jnp.bfloat16)
    load_cot.wait()
    load_w.wait()
    back = nt_dot(cot_buf[...], w_buf[...]).astype(jnp.bfloat16)
    back_ref[...] = back
    half = SLOTS * TILE
    up_ref[...] = tn_dot(fold_ref[:, :half], back).astype(jnp.bfloat16).reshape(up_ref.shape)
    down_ref[...] = tn_dot(fold_ref[:, half:], back).astype(jnp.bfloat16).reshape(down_ref.shape)


def near_kernel(adj_ref, src_ref, back_ref, after_ref, fold_ref, up_ref, down_ref, acc_ref):
    acc_ref[...] = jnp.zeros_like(acc_ref)
    for seed in range(adj_ref.shape[0]):
        rows = pl.ds(seed * TILE, TILE)

        def add(k, _):
            slot = src_ref[seed, k]
            local = slot < TILE_DEV
            near = (slot >= TILE_DEV + SLOTS) & (slot < TILE_DEV + 3 * SLOTS)

            @pl.when(local | near)
            def _():
                at = jnp.where(local, slot, slot - SLOTS)
                cols = pl.ds(pl.multiple_of(at * TILE, TILE), TILE)
                acc_ref[rows, cols] += adj_ref[seed, k].astype(jnp.float32)

            return 0

        lax.fori_loop(0, adj_ref.shape[1], add, 0, unroll=4)
    fold_ref[...] = acc_ref[...].astype(jnp.bfloat16)
    back = back_ref[...]
    start, half = TILE_DEV * TILE, SLOTS * TILE
    up_ref[...] = tn_dot(fold_ref[:, start : start + half], back).astype(jnp.bfloat16).reshape(up_ref.shape)
    down_ref[...] = tn_dot(fold_ref[:, start + half :], back).astype(jnp.bfloat16).reshape(down_ref.shape)


def local_kernel(fold_ref, back_ref, cot_ref, w_ref, seeds_ref, after_up_ref, after_down_ref, out_ref):
    rows = out_ref.shape[0]
    back_self = nt_dot(cot_ref[...], w_ref[...]).astype(jnp.bfloat16)
    hot = lax.broadcasted_iota(jnp.int32, (rows, seeds_ref.shape[1]), 0) == seeds_ref[...]
    hot = hot.astype(jnp.float32).astype(jnp.bfloat16)
    out_ref[...] = nn_dot(hot, back_self) + tn_dot(fold_ref[:, :rows], back_ref[...])


def gather_kernel(src_ref, feat_ref, adj_ref, after_ref, out_ref):
    step = pl.program_id(0)
    width = feat_ref.shape[0]
    span = out_ref.shape[2]
    out_ref[0, :width] = feat_ref[:, pl.ds(pl.multiple_of(step * span, span), span)]
    for tile in range(adj_ref.shape[0]):
        parts = []
        for k in range(adj_ref.shape[1]):
            source = src_ref[k, step * adj_ref.shape[0] + tile]
            parts.append(feat_ref[:, pl.ds(pl.multiple_of(source * TILE, TILE), TILE)])
        left = jnp.concatenate(parts, axis=1)
        right = jnp.concatenate([adj_ref[tile, k] for k in range(adj_ref.shape[1])], axis=1)
        out_ref[0, width:, tile * TILE : (tile + 1) * TILE] = nt_dot(left, right).astype(jnp.bfloat16)


def hidden_kernel(
    in_ref, mine_ref, other_ref, bias_ref, odd_ref, tiles_ref, count_ref, after_ref,
    hid_ref, up_ref, down_ref, turned_ref,
):
    slices, width, span = in_ref.shape[0], in_ref.shape[1] // 2, in_ref.shape[2]
    depth = slices * width

    @pl.when(pl.program_id(0) == 0)
    def _():
        for half, odd in enumerate((odd_ref[0], 1 - odd_ref[0])):
            kind = in_ref[:, pl.ds(pl.multiple_of(odd * width, width), width)]
            turned_ref[:, half * depth : (half + 1) * depth] = kind.reshape(depth, span).T

    total = nn_dot(turned_ref[:, :depth], mine_ref[...]) + nn_dot(turned_ref[:, depth:], other_ref[...])
    hidden = jnp.maximum(total + bias_ref[...], 0.0).astype(jnp.bfloat16)
    hid_ref[...] = hidden.reshape(hid_ref.shape)
    shape = (2 * ROWS, up_ref.shape[1])
    row = lax.broadcasted_iota(jnp.int32, shape, 0)
    block = (lax.broadcasted_iota(jnp.int32, shape, 1) + pl.program_id(0) * shape[1]) // TILE
    for near_q, far_q, out_ref in ((2, 3, up_ref), (1, 0, down_ref)):
        places = order_of(lambda m: tiles_ref[far_q, m], count_ref[far_q])
        for tile in range(TILE_DEV):

            @pl.when(places[tile] < NEAR)
            def _():
                at = jnp.minimum(places[tile], NEAR - 1) * TILE
                out_ref[pl.ds(pl.multiple_of(at, TILE), TILE)] = hid_ref[tile]

        marks = jnp.zeros(shape, jnp.float32)
        for first, q in ((0, near_q), (SLOTS, far_q)):
            for slot in range(SLOTS):
                at = jnp.where(slot < count_ref[q], place_of(places, tiles_ref[q, slot]), -1)
                marks = jnp.where((row == first + slot) & (block == at), 1.0, marks)
        out_ref[NEAR * TILE :] = marks.astype(jnp.bfloat16)


def merge_kernel(
    local_ref, from_0_ref, from_1_ref, from_2_ref, from_3_ref, hid_ref, tiles_ref, count_ref,
    out_ref, rest_up_ref, rest_down_ref,
):
    out_ref[...] = local_ref[...]
    for q, ref in enumerate((from_0_ref, from_1_ref, from_2_ref, from_3_ref)):
        for slot in range(SLOTS):

            @pl.when(slot < count_ref[q])
            def _():
                at = pl.multiple_of(tiles_ref[q, slot] * TILE, TILE)
                out_ref[pl.ds(at, TILE)] += ref[slot].astype(jnp.float32)

    for far_q, rest_ref in ((3, rest_up_ref), (0, rest_down_ref)):
        places = order_of(lambda m: tiles_ref[far_q, m], count_ref[far_q])
        for tile in range(TILE_DEV):

            @pl.when(places[tile] >= NEAR)
            def _():
                rest_ref[jnp.maximum(places[tile] - NEAR, 0)] = hid_ref[tile]


def placed(fold_ref, start, mark_ref, first, count, out_ref, to):
    marks = mark_ref[NEAR * TILE :].astype(jnp.float32)
    blocks = [
        fold_ref[:, (start + slot) * TILE : (start + slot + 1) * TILE].astype(jnp.float32) for slot in range(SLOTS)
    ]
    for place in range(count):
        cols = slice(place * TILE, (place + 1) * TILE)
        total = sum(blocks[slot] * marks[first + slot : first + slot + 1, cols] for slot in range(SLOTS))
        out_ref[:, (to + place) * TILE : (to + place + 1) * TILE] = total.astype(jnp.bfloat16)


def mid_kernel(
    fold_ref, hid_ref, a_up_ref, rest_up_ref, a_down_ref, rest_down_ref, seeds_ref, w_ref, bias_ref,
    part_ref, self_ref, placed_ref, table_ref,
):
    rows = TILE_DEV * TILE
    quad = NEAR * TILE
    pair = rows - quad
    hidden = hid_ref[...].reshape(rows, hid_ref.shape[2])
    start = 0
    for first, a_ref, rest_ref in ((TILE_DEV, a_down_ref, rest_down_ref), (TILE_DEV + SLOTS, a_up_ref, rest_up_ref)):
        placed(fold_ref, first, a_ref, 0, TILE_DEV, placed_ref, start // TILE)
        table_ref[start : start + quad] = a_ref[:quad]
        table_ref[start + quad : start + rows] = rest_ref[...].reshape(pair, rest_ref.shape[2])
        start += rows
    part_ref[...] = nn_dot(fold_ref[:, :rows], hidden) + nn_dot(placed_ref[...], table_ref[...])
    hot = lax.broadcasted_iota(jnp.int32, (rows, seeds_ref.shape[1]), 0) == seeds_ref[...]
    hot = hot.astype(jnp.float32).astype(jnp.bfloat16)
    chosen = tn_dot(hot, hidden).astype(jnp.bfloat16)
    self_ref[...] = nn_dot(chosen, w_ref[...]) + bias_ref[...]


def last_kernel(fold_ref, f_up_ref, f_down_ref, part_ref, self_ref, w_ref, out_ref, placed_ref):
    quad = NEAR * TILE
    placed(fold_ref, 0, f_down_ref, SLOTS, NEAR, placed_ref, 0)
    placed(fold_ref, SLOTS, f_up_ref, SLOTS, NEAR, placed_ref, NEAR)
    gathered = part_ref[...] + nn_dot(placed_ref[:, :quad], f_down_ref[:quad])
    gathered = (gathered + nn_dot(placed_ref[:, quad:], f_up_ref[:quad])).astype(jnp.bfloat16)
    out_ref[...] = (self_ref[...] + nn_dot(gathered, w_ref[...])).astype(jnp.bfloat16)


def shards(
    features,
    adj_one,
    src_one,
    w_self_one,
    w_neigh_one,
    bias_one,
    w_self_two,
    w_neigh_two,
    bias_two,
    seed_rows,
    adj_two,
    src_two,
    send_tiles,
    send_count,
    cotangent,
):
    bf16, f32 = jnp.bfloat16, jnp.float32
    width = features.shape[0]
    part_tiles = adj_one.shape[0]
    hid = w_self_two.shape[0]
    feat_count = lax.axis_size("feat")
    row_dev = features.shape[1] // feat_count
    seeds = cotangent.shape[1]
    blocks, sources = adj_two[0, 0], src_two[0, 0]
    upstream = cotangent[0]
    shape = jax.ShapeDtypeStruct

    lists = send_tiles[0, 0]
    partner = lax.axis_index("dom") + jnp.array(OFFSETS, jnp.int32)
    inside = (partner >= 0) & (partner < lax.axis_size("dom"))
    counts = jnp.where(inside, send_count[0, 0], 0)
    quad = shape((NEAR, TILE, hid), bf16)
    pair = shape((TILE_DEV - NEAR, TILE, hid), bf16)
    quad_marked = shape((NEAR * TILE + 2 * ROWS, hid), bf16)
    far_cols, near_cols = 2 * SLOTS * TILE, (TILE_DEV + 2 * SLOTS) * TILE

    back, fold_far, far_up, far_down = call(
        far_kernel,
        (shape((seeds, hid), bf16), shape((seeds, far_cols), bf16), quad, quad),
        [ANY, SMEM, ANY, ANY],
        [
            pltpu.VMEM(blocks.shape, bf16),
            pltpu.VMEM((seeds, hid), bf16),
            pltpu.VMEM((hid, hid), bf16),
            pltpu.VMEM((seeds, far_cols), f32),
            pltpu.SemaphoreType.DMA((blocks.shape[0] + 2,)),
        ],
        vmem=56,
            )(blocks, sources, upstream, w_neigh_two)
    halves = call(
        halves_kernel,
        shape((feat_count, width, hid), bf16),
        [ANY, ANY, ANY],
        [pltpu.VMEM((2, width, hid), bf16), pltpu.SemaphoreType.DMA((2 + feat_count,))],
        vmem=56,
        out_specs=ANY,
    )(w_self_one, w_neigh_one, far_up)
    halves = lax.all_to_all(halves, "feat", 0, 0)
    halves = halves.reshape(feat_count * width, hid)
    got_far_up = shifted(far_up, 1)
    got_far_down = shifted(far_down, -1)

    sent = pl.pallas_call(
        gather_kernel,
        grid=(feat_count,),
        in_specs=[
            SMEM,
            pl.BlockSpec((width, features.shape[1]), lambda i: (0, 0)),
            pl.BlockSpec((part_tiles // feat_count,) + adj_one.shape[1:], lambda i: (i, 0, 0, 0)),
            ANY,
        ],
        out_specs=pl.BlockSpec((1, 2 * width, row_dev), lambda i: (i, 0, 0)),
        out_shape=shape((feat_count, 2 * width, row_dev), bf16),
        cost_estimate=pl.CostEstimate(flops=100 * GIGA, bytes_accessed=1, transcendentals=0),
        compiler_params=pltpu.CompilerParams(vmem_limit_bytes=56 * MIB),
    )(src_one.T, features, adj_one, back)
    taken = lax.all_to_all(sent, "feat", 0, 0)
    swapped = lax.ppermute(halves, "feat", [(i, i ^ 1) for i in range(feat_count)])
    odd = (lax.axis_index("feat") % 2).astype(jnp.int32)[None]

    fold_near, near_up, near_down = call(
        near_kernel,
        (shape((seeds, near_cols), bf16), quad, quad),
        [VMEM, SMEM, VMEM, ANY],
        [pltpu.VMEM((seeds, near_cols), f32)],
        vmem=24,
    )(blocks, sources, back, sent)
    grad_1 = shifted(near_up, 1)
    grad_2 = shifted(near_down, -1)
    grad_0 = shifted(got_far_up, 1)
    grad_3 = shifted(got_far_down, -1)

    local = call(
        local_kernel,
        shape((row_dev, hid), f32),
        [VMEM] * 5 + [ANY] * 2,
        cost=20,
        vmem=28,
    )(fold_near, back, upstream, w_self_two, seed_rows[0], got_far_up, got_far_down)

    chunk = hid // 2
    hidden, h_up, h_down = pl.pallas_call(
        hidden_kernel,
        grid=(hid // chunk,),
        in_specs=[
            pl.BlockSpec(taken.shape, lambda j: (0, 0, 0)),
            pl.BlockSpec((feat_count * width, chunk), lambda j: (0, j)),
            pl.BlockSpec((feat_count * width, chunk), lambda j: (0, j)),
            pl.BlockSpec((1, chunk), lambda j: (0, j)),
            SMEM,
            SMEM,
            SMEM,
            ANY,
        ],
        out_specs=[
            pl.BlockSpec((TILE_DEV, TILE, chunk), lambda j: (0, 0, j)),
            pl.BlockSpec((quad_marked.shape[0], chunk), lambda j: (0, j)),
            pl.BlockSpec((quad_marked.shape[0], chunk), lambda j: (0, j)),
        ],
        out_shape=(shape((TILE_DEV, TILE, hid), bf16), quad_marked, quad_marked),
        scratch_shapes=[
            pltpu.VMEM((row_dev, 2 * width * feat_count), bf16),
        ],
        cost_estimate=pl.CostEstimate(flops=GIGA, bytes_accessed=1, transcendentals=0),
        compiler_params=pltpu.CompilerParams(vmem_limit_bytes=24 * MIB),
    )(taken, halves, swapped, bias_one[None], odd, lists, counts, local)
    got_h_up = shifted(h_up, 1)
    got_h_down = shifted(h_down, -1)
    next_up = open_shift(got_h_up, 1)
    next_down = open_shift(got_h_down, -1)
    grads, rest_up, rest_down = call(
        merge_kernel, (shape((row_dev, hid), f32), pair, pair), [VMEM] * 6 + [SMEM] * 2, vmem=24
    )(local, grad_0, grad_1, grad_2, grad_3, hidden, lists, counts)
    got_rest_up = shifted(rest_up, 1)
    got_rest_down = shifted(rest_down, -1)

    part, self_term = call(
        mid_kernel,
        (shape((seeds, hid), f32), shape((seeds, hid), f32)),
        [VMEM] * 9,
        [pltpu.VMEM((seeds, 2 * row_dev), bf16), pltpu.VMEM((2 * row_dev, hid), bf16)],
        cost=100,
        vmem=32,
    )(
        fold_near, hidden, got_h_up, got_rest_up, got_h_down, got_rest_down,
        seed_rows[0], w_self_two, bias_two[None],
    )
    layer_out = call(
        last_kernel,
        shape((seeds, hid), bf16),
        [VMEM] * 6,
        [pltpu.VMEM((seeds, far_cols), bf16)],
        vmem=20,
    )(fold_far, next_up, next_down, part, self_term, w_neigh_two)
    return (layer_out[None], grads[None])


def solution(mesh):
    return jax.shard_map(
        shards,
        mesh=mesh,
        in_specs=(
            P("feat", "dom"),
            P("dom", None, None, None),
            P("dom", None),
            P("feat", None),
            P("feat", None),
            P(),
            P(),
            P(),
            P(),
            P("dom", "feat", None),
            P("dom", "feat", None, None, None, None),
            P("dom", "feat", None, None),
            P("dom", "feat", None, None),
            P("dom", "feat", None),
            P("dom", "feat", None),
        ),
        out_specs=(P("dom", "feat", None), P("dom", "feat", None)),
        check_vma=False,
    )
```

```python
import functools

import jax
import jax.numpy as jnp
from jax import lax
from jax.experimental import pallas as pl
from jax.experimental.pallas import tpu as pltpu
from jax.sharding import PartitionSpec as P

TILE = 128
TILE_DEV = 6
SLOTS = 4
NEAR = 4
ROWS = 8
MIB = 1 << 20
OFFSETS = (-2, -1, 1, 2)
GIGA = 1 << 30

VMEM = pl.BlockSpec(memory_space=pltpu.VMEM)
SMEM = pl.BlockSpec(memory_space=pltpu.SMEM)
ANY = pl.BlockSpec(memory_space=pl.ANY)


def open_shift(shard, by):
    count = lax.axis_size("dom")
    return lax.ppermute(shard, "dom", [(i, i + by) for i in range(count) if 0 <= i + by < count])


def shifted(shard, by):
    count = lax.axis_size("dom")
    return lax.ppermute(shard, "dom", [(i, (i + by) % count) for i in range(count)])


def call(body, outs, in_specs, scratch=(), cost=1, vmem=32, out_specs=None):
    return pl.pallas_call(
        body,
        out_shape=outs,
        in_specs=in_specs,
        out_specs=out_specs or jax.tree.map(lambda _: VMEM, outs),
        scratch_shapes=list(scratch),
        cost_estimate=pl.CostEstimate(flops=cost * GIGA, bytes_accessed=1, transcendentals=0),
        compiler_params=pltpu.CompilerParams(vmem_limit_bytes=vmem * MIB),
    )


def tn_dot(left, right):
    return lax.dot_general(left, right, (((0,), (0,)), ((), ())), preferred_element_type=jnp.float32)


def nt_dot(left, right):
    return lax.dot_general(left, right, (((1,), (1,)), ((), ())), preferred_element_type=jnp.float32)


def nn_dot(left, right):
    return jnp.dot(left, right, preferred_element_type=jnp.float32)


def order_of(tiles, count):
    listed = []
    for tile in range(TILE_DEV):
        hit = jnp.int32(0)
        for slot in range(SLOTS):
            hit = jnp.where((tiles(slot) == tile) & (slot < count), 1, hit)
        listed.append(hit)
    total = functools.reduce(lambda a, b: a + b, listed)
    places = []
    ahead = jnp.int32(0)
    behind = total
    for tile in range(TILE_DEV):
        places.append(jnp.where(listed[tile] == 1, ahead, behind))
        ahead = ahead + listed[tile]
        behind = behind + (1 - listed[tile])
    return places


def place_of(places, tile):
    at = places[0]
    for other in range(1, TILE_DEV):
        at = jnp.where(tile == other, places[other], at)
    return at


def halves_kernel(self_ref, neigh_ref, after_ref, out_ref, buf, sems):
    loads = [pltpu.make_async_copy(ref, buf.at[i], sems.at[i]) for i, ref in enumerate((self_ref, neigh_ref))]
    stores = [pltpu.make_async_copy(buf.at[i % 2], out_ref.at[i], sems.at[2 + i]) for i in range(out_ref.shape[0])]
    for load in loads:
        load.start()
    for kind, load in enumerate(loads):
        load.wait()
        for store in stores[kind::2]:
            store.start()
    for store in stores:
        store.wait()


def far_kernel(
    adj_ref, src_ref, cot_ref, w_ref,
    back_ref, fold_ref, up_ref, down_ref, adj_buf, cot_buf, w_buf, acc_ref, sems,
):
    seeds = adj_ref.shape[0]
    loads = [pltpu.make_async_copy(adj_ref.at[s], adj_buf.at[s], sems.at[s]) for s in range(seeds)]
    load_w = pltpu.make_async_copy(w_ref, w_buf, sems.at[seeds])
    load_cot = pltpu.make_async_copy(cot_ref, cot_buf, sems.at[seeds + 1])
    for load in loads:
        load.start()
    load_cot.start()
    load_w.start()
    acc_ref[...] = jnp.zeros_like(acc_ref)
    for seed in range(seeds):
        loads[seed].wait()
        rows = pl.ds(seed * TILE, TILE)

        def add(k, _):
            slot = src_ref[seed, k] - TILE_DEV
            low = (slot >= 0) & (slot < SLOTS)
            high = slot >= 3 * SLOTS

            @pl.when(low | high)
            def _():
                at = jnp.where(low, slot, slot - 2 * SLOTS)
                cols = pl.ds(pl.multiple_of(at * TILE, TILE), TILE)
                acc_ref[rows, cols] += adj_buf[seed, k].astype(jnp.float32)

            return 0

        lax.fori_loop(0, adj_ref.shape[1], add, 0, unroll=4)
    fold_ref[...] = acc_ref[...].astype(jnp.bfloat16)
    load_cot.wait()
    load_w.wait()
    back = nt_dot(cot_buf[...], w_buf[...]).astype(jnp.bfloat16)
    back_ref[...] = back
    half = SLOTS * TILE
    up_ref[...] = tn_dot(fold_ref[:, :half], back).astype(jnp.bfloat16).reshape(up_ref.shape)
    down_ref[...] = tn_dot(fold_ref[:, half:], back).astype(jnp.bfloat16).reshape(down_ref.shape)


def near_kernel(adj_ref, src_ref, back_ref, fold_ref, up_ref, down_ref, acc_ref):
    acc_ref[...] = jnp.zeros_like(acc_ref)
    for seed in range(adj_ref.shape[0]):
        rows = pl.ds(seed * TILE, TILE)

        def add(k, _):
            slot = src_ref[seed, k]
            local = slot < TILE_DEV
            near = (slot >= TILE_DEV + SLOTS) & (slot < TILE_DEV + 3 * SLOTS)

            @pl.when(local | near)
            def _():
                at = jnp.where(local, slot, slot - SLOTS)
                cols = pl.ds(pl.multiple_of(at * TILE, TILE), TILE)
                acc_ref[rows, cols] += adj_ref[seed, k].astype(jnp.float32)

            return 0

        lax.fori_loop(0, adj_ref.shape[1], add, 0, unroll=4)
    fold_ref[...] = acc_ref[...].astype(jnp.bfloat16)
    back = back_ref[...]
    start, half = TILE_DEV * TILE, SLOTS * TILE
    up_ref[...] = tn_dot(fold_ref[:, start : start + half], back).astype(jnp.bfloat16).reshape(up_ref.shape)
    down_ref[...] = tn_dot(fold_ref[:, start + half :], back).astype(jnp.bfloat16).reshape(down_ref.shape)


def local_kernel(fold_ref, back_ref, cot_ref, w_ref, seeds_ref, after_up_ref, after_down_ref, out_ref):
    rows = out_ref.shape[0]
    back_self = nt_dot(cot_ref[...], w_ref[...]).astype(jnp.bfloat16)
    hot = lax.broadcasted_iota(jnp.int32, (rows, seeds_ref.shape[1]), 0) == seeds_ref[...]
    hot = hot.astype(jnp.float32).astype(jnp.bfloat16)
    out_ref[...] = nn_dot(hot, back_self) + tn_dot(fold_ref[:, :rows], back_ref[...])


def gather_kernel(src_ref, feat_ref, adj_ref, after_ref, out_ref):
    step = pl.program_id(0)
    width = feat_ref.shape[0]
    span = out_ref.shape[2]
    out_ref[0, :width] = feat_ref[:, pl.ds(pl.multiple_of(step * span, span), span)]
    for tile in range(adj_ref.shape[0]):
        parts = []
        for k in range(adj_ref.shape[1]):
            source = src_ref[k, step * adj_ref.shape[0] + tile]
            parts.append(feat_ref[:, pl.ds(pl.multiple_of(source * TILE, TILE), TILE)])
        left = jnp.concatenate(parts, axis=1)
        right = jnp.concatenate([adj_ref[tile, k] for k in range(adj_ref.shape[1])], axis=1)
        out_ref[0, width:, tile * TILE : (tile + 1) * TILE] = nt_dot(left, right).astype(jnp.bfloat16)


def hidden_kernel(
    in_ref, mine_ref, other_ref, bias_ref, odd_ref, tiles_ref, count_ref, after_ref,
    hid_ref, up_ref, down_ref, turned_ref,
):
    slices, width, span = in_ref.shape[0], in_ref.shape[1] // 2, in_ref.shape[2]
    depth = slices * width

    @pl.when(pl.program_id(0) == 0)
    def _():
        for half, odd in enumerate((odd_ref[0], 1 - odd_ref[0])):
            kind = in_ref[:, pl.ds(pl.multiple_of(odd * width, width), width)]
            turned_ref[:, half * depth : (half + 1) * depth] = kind.reshape(depth, span).T

    total = nn_dot(turned_ref[:, :depth], mine_ref[...]) + nn_dot(turned_ref[:, depth:], other_ref[...])
    hidden = jnp.maximum(total + bias_ref[...], 0.0).astype(jnp.bfloat16)
    hid_ref[...] = hidden.reshape(hid_ref.shape)
    shape = (2 * ROWS, up_ref.shape[1])
    row = lax.broadcasted_iota(jnp.int32, shape, 0)
    block = (lax.broadcasted_iota(jnp.int32, shape, 1) + pl.program_id(0) * shape[1]) // TILE
    for near_q, far_q, out_ref in ((2, 3, up_ref), (1, 0, down_ref)):
        places = order_of(lambda m: tiles_ref[far_q, m], count_ref[far_q])
        for tile in range(TILE_DEV):

            @pl.when(places[tile] < NEAR)
            def _():
                at = jnp.minimum(places[tile], NEAR - 1) * TILE
                out_ref[pl.ds(pl.multiple_of(at, TILE), TILE)] = hid_ref[tile]

        marks = jnp.zeros(shape, jnp.float32)
        for first, q in ((0, near_q), (SLOTS, far_q)):
            for slot in range(SLOTS):
                at = jnp.where(slot < count_ref[q], place_of(places, tiles_ref[q, slot]), -1)
                marks = jnp.where((row == first + slot) & (block == at), 1.0, marks)
        out_ref[NEAR * TILE :] = marks.astype(jnp.bfloat16)


def merge_kernel(
    local_ref, from_0_ref, from_1_ref, from_2_ref, from_3_ref, hid_ref, tiles_ref, count_ref,
    out_ref, rest_up_ref, rest_down_ref,
):
    out_ref[...] = local_ref[...]
    for q, ref in enumerate((from_0_ref, from_1_ref, from_2_ref, from_3_ref)):
        for slot in range(SLOTS):

            @pl.when(slot < count_ref[q])
            def _():
                at = pl.multiple_of(tiles_ref[q, slot] * TILE, TILE)
                out_ref[pl.ds(at, TILE)] += ref[slot].astype(jnp.float32)

    for far_q, rest_ref in ((3, rest_up_ref), (0, rest_down_ref)):
        places = order_of(lambda m: tiles_ref[far_q, m], count_ref[far_q])
        for tile in range(TILE_DEV):

            @pl.when(places[tile] >= NEAR)
            def _():
                rest_ref[jnp.maximum(places[tile] - NEAR, 0)] = hid_ref[tile]


def placed(fold_ref, start, mark_ref, first, count, out_ref, to):
    marks = mark_ref[NEAR * TILE :].astype(jnp.float32)
    blocks = [
        fold_ref[:, (start + slot) * TILE : (start + slot + 1) * TILE].astype(jnp.float32) for slot in range(SLOTS)
    ]
    for place in range(count):
        cols = slice(place * TILE, (place + 1) * TILE)
        total = sum(blocks[slot] * marks[first + slot : first + slot + 1, cols] for slot in range(SLOTS))
        out_ref[:, (to + place) * TILE : (to + place + 1) * TILE] = total.astype(jnp.bfloat16)


def mid_kernel(
    fold_ref, hid_ref, a_up_ref, rest_up_ref, a_down_ref, rest_down_ref, seeds_ref, w_ref, bias_ref,
    part_ref, self_ref, placed_ref, table_ref,
):
    rows = TILE_DEV * TILE
    quad = NEAR * TILE
    pair = rows - quad
    hidden = hid_ref[...].reshape(rows, hid_ref.shape[2])
    start = 0
    for first, a_ref, rest_ref in ((TILE_DEV, a_down_ref, rest_down_ref), (TILE_DEV + SLOTS, a_up_ref, rest_up_ref)):
        placed(fold_ref, first, a_ref, 0, TILE_DEV, placed_ref, start // TILE)
        table_ref[start : start + quad] = a_ref[:quad]
        table_ref[start + quad : start + rows] = rest_ref[...].reshape(pair, rest_ref.shape[2])
        start += rows
    part_ref[...] = nn_dot(fold_ref[:, :rows], hidden) + nn_dot(placed_ref[...], table_ref[...])
    hot = lax.broadcasted_iota(jnp.int32, (rows, seeds_ref.shape[1]), 0) == seeds_ref[...]
    hot = hot.astype(jnp.float32).astype(jnp.bfloat16)
    chosen = tn_dot(hot, hidden).astype(jnp.bfloat16)
    self_ref[...] = nn_dot(chosen, w_ref[...]) + bias_ref[...]


def last_kernel(fold_ref, f_up_ref, f_down_ref, part_ref, self_ref, w_ref, out_ref, placed_ref):
    quad = NEAR * TILE
    placed(fold_ref, 0, f_down_ref, SLOTS, NEAR, placed_ref, 0)
    placed(fold_ref, SLOTS, f_up_ref, SLOTS, NEAR, placed_ref, NEAR)
    gathered = part_ref[...] + nn_dot(placed_ref[:, :quad], f_down_ref[:quad])
    gathered = (gathered + nn_dot(placed_ref[:, quad:], f_up_ref[:quad])).astype(jnp.bfloat16)
    out_ref[...] = (self_ref[...] + nn_dot(gathered, w_ref[...])).astype(jnp.bfloat16)


def shards(
    features,
    adj_one,
    src_one,
    w_self_one,
    w_neigh_one,
    bias_one,
    w_self_two,
    w_neigh_two,
    bias_two,
    seed_rows,
    adj_two,
    src_two,
    send_tiles,
    send_count,
    cotangent,
):
    bf16, f32 = jnp.bfloat16, jnp.float32
    width = features.shape[0]
    part_tiles = adj_one.shape[0]
    hid = w_self_two.shape[0]
    feat_count = lax.axis_size("feat")
    row_dev = features.shape[1] // feat_count
    seeds = cotangent.shape[1]
    blocks, sources = adj_two[0, 0], src_two[0, 0]
    upstream = cotangent[0]
    shape = jax.ShapeDtypeStruct

    lists = send_tiles[0, 0]
    partner = lax.axis_index("dom") + jnp.array(OFFSETS, jnp.int32)
    inside = (partner >= 0) & (partner < lax.axis_size("dom"))
    counts = jnp.where(inside, send_count[0, 0], 0)
    quad = shape((NEAR, TILE, hid), bf16)
    pair = shape((TILE_DEV - NEAR, TILE, hid), bf16)
    quad_marked = shape((NEAR * TILE + 2 * ROWS, hid), bf16)
    far_cols, near_cols = 2 * SLOTS * TILE, (TILE_DEV + 2 * SLOTS) * TILE

    back, fold_far, far_up, far_down = call(
        far_kernel,
        (shape((seeds, hid), bf16), shape((seeds, far_cols), bf16), quad, quad),
        [ANY, SMEM, ANY, ANY],
        [
            pltpu.VMEM(blocks.shape, bf16),
            pltpu.VMEM((seeds, hid), bf16),
            pltpu.VMEM((hid, hid), bf16),
            pltpu.VMEM((seeds, far_cols), f32),
            pltpu.SemaphoreType.DMA((blocks.shape[0] + 2,)),
        ],
        vmem=56,
            )(blocks, sources, upstream, w_neigh_two)
    halves = call(
        halves_kernel,
        shape((feat_count, width, hid), bf16),
        [ANY, ANY, ANY],
        [pltpu.VMEM((2, width, hid), bf16), pltpu.SemaphoreType.DMA((2 + feat_count,))],
        vmem=56,
        out_specs=ANY,
    )(w_self_one, w_neigh_one, far_up)
    halves = lax.all_to_all(halves, "feat", 0, 0)
    halves = halves.reshape(feat_count * width, hid)
    got_far_up = shifted(far_up, 1)
    got_far_down = shifted(far_down, -1)

    fold_near, near_up, near_down = call(
        near_kernel,
        (shape((seeds, near_cols), bf16), quad, quad),
        [VMEM, SMEM, VMEM],
        [pltpu.VMEM((seeds, near_cols), f32)],
        vmem=24,
    )(blocks, sources, back)

    sent = pl.pallas_call(
        gather_kernel,
        grid=(feat_count,),
        in_specs=[
            SMEM,
            pl.BlockSpec((width, features.shape[1]), lambda i: (0, 0)),
            pl.BlockSpec((part_tiles // feat_count,) + adj_one.shape[1:], lambda i: (i, 0, 0, 0)),
            ANY,
        ],
        out_specs=pl.BlockSpec((1, 2 * width, row_dev), lambda i: (i, 0, 0)),
        out_shape=shape((feat_count, 2 * width, row_dev), bf16),
        cost_estimate=pl.CostEstimate(flops=100 * GIGA, bytes_accessed=1, transcendentals=0),
        compiler_params=pltpu.CompilerParams(vmem_limit_bytes=56 * MIB),
    )(src_one.T, features, adj_one, near_up)
    taken = lax.all_to_all(sent, "feat", 0, 0)
    swapped = lax.ppermute(halves, "feat", [(i, i ^ 1) for i in range(feat_count)])
    odd = (lax.axis_index("feat") % 2).astype(jnp.int32)[None]

    grad_1 = shifted(near_up, 1)
    grad_2 = shifted(near_down, -1)
    grad_0 = shifted(got_far_up, 1)
    grad_3 = shifted(got_far_down, -1)

    local = call(
        local_kernel,
        shape((row_dev, hid), f32),
        [VMEM] * 5 + [ANY] * 2,
        cost=20,
        vmem=28,
    )(fold_near, back, upstream, w_self_two, seed_rows[0], got_far_up, got_far_down)

    chunk = hid
    hidden, h_up, h_down = pl.pallas_call(
        hidden_kernel,
        grid=(hid // chunk,),
        in_specs=[
            pl.BlockSpec(taken.shape, lambda j: (0, 0, 0)),
            pl.BlockSpec((feat_count * width, chunk), lambda j: (0, j)),
            pl.BlockSpec((feat_count * width, chunk), lambda j: (0, j)),
            pl.BlockSpec((1, chunk), lambda j: (0, j)),
            SMEM,
            SMEM,
            SMEM,
            ANY,
        ],
        out_specs=[
            pl.BlockSpec((TILE_DEV, TILE, chunk), lambda j: (0, 0, j)),
            pl.BlockSpec((quad_marked.shape[0], chunk), lambda j: (0, j)),
            pl.BlockSpec((quad_marked.shape[0], chunk), lambda j: (0, j)),
        ],
        out_shape=(shape((TILE_DEV, TILE, hid), bf16), quad_marked, quad_marked),
        scratch_shapes=[
            pltpu.VMEM((row_dev, 2 * width * feat_count), bf16),
        ],
        cost_estimate=pl.CostEstimate(flops=GIGA, bytes_accessed=1, transcendentals=0),
        compiler_params=pltpu.CompilerParams(vmem_limit_bytes=30 * MIB),
    )(taken, halves, swapped, bias_one[None], odd, lists, counts, local)
    got_h_up = shifted(h_up, 1)
    got_h_down = shifted(h_down, -1)
    next_up = open_shift(got_h_up, 1)
    next_down = open_shift(got_h_down, -1)
    grads, rest_up, rest_down = call(
        merge_kernel, (shape((row_dev, hid), f32), pair, pair), [VMEM] * 6 + [SMEM] * 2, vmem=24
    )(local, grad_0, grad_1, grad_2, grad_3, hidden, lists, counts)
    got_rest_up = shifted(rest_up, 1)
    got_rest_down = shifted(rest_down, -1)

    part, self_term = call(
        mid_kernel,
        (shape((seeds, hid), f32), shape((seeds, hid), f32)),
        [VMEM] * 9,
        [pltpu.VMEM((seeds, 2 * row_dev), bf16), pltpu.VMEM((2 * row_dev, hid), bf16)],
        cost=100,
        vmem=32,
    )(
        fold_near, hidden, got_h_up, got_rest_up, got_h_down, got_rest_down,
        seed_rows[0], w_self_two, bias_two[None],
    )
    layer_out = call(
        last_kernel,
        shape((seeds, hid), bf16),
        [VMEM] * 6,
        [pltpu.VMEM((seeds, far_cols), bf16)],
        vmem=20,
    )(fold_far, next_up, next_down, part, self_term, w_neigh_two)
    return (layer_out[None], grads[None])


def solution(mesh):
    return jax.shard_map(
        shards,
        mesh=mesh,
        in_specs=(
            P("feat", "dom"),
            P("dom", None, None, None),
            P("dom", None),
            P("feat", None),
            P("feat", None),
            P(),
            P(),
            P(),
            P(),
            P("dom", "feat", None),
            P("dom", "feat", None, None, None, None),
            P("dom", "feat", None, None),
            P("dom", "feat", None, None),
            P("dom", "feat", None),
            P("dom", "feat", None),
        ),
        out_specs=(P("dom", "feat", None), P("dom", "feat", None)),
        check_vma=False,
    )
```

```python
import functools

import jax
import jax.numpy as jnp
from jax import lax
from jax.experimental import pallas as pl
from jax.experimental.pallas import tpu as pltpu
from jax.sharding import PartitionSpec as P

TILE = 128
TILE_DEV = 6
SLOTS = 4
NEAR = 4
ROWS = 8
MIB = 1 << 20
OFFSETS = (-2, -1, 1, 2)
GIGA = 1 << 30

VMEM = pl.BlockSpec(memory_space=pltpu.VMEM)
SMEM = pl.BlockSpec(memory_space=pltpu.SMEM)
ANY = pl.BlockSpec(memory_space=pl.ANY)


def open_shift(shard, by):
    count = lax.axis_size("dom")
    return lax.ppermute(shard, "dom", [(i, i + by) for i in range(count) if 0 <= i + by < count])


def shifted(shard, by):
    count = lax.axis_size("dom")
    return lax.ppermute(shard, "dom", [(i, (i + by) % count) for i in range(count)])


def call(body, outs, in_specs, scratch=(), cost=1, vmem=32, out_specs=None):
    return pl.pallas_call(
        body,
        out_shape=outs,
        in_specs=in_specs,
        out_specs=out_specs or jax.tree.map(lambda _: VMEM, outs),
        scratch_shapes=list(scratch),
        cost_estimate=pl.CostEstimate(flops=cost * GIGA, bytes_accessed=1, transcendentals=0),
        compiler_params=pltpu.CompilerParams(vmem_limit_bytes=vmem * MIB),
    )


def tn_dot(left, right):
    return lax.dot_general(left, right, (((0,), (0,)), ((), ())), preferred_element_type=jnp.float32)


def nt_dot(left, right):
    return lax.dot_general(left, right, (((1,), (1,)), ((), ())), preferred_element_type=jnp.float32)


def nn_dot(left, right):
    return jnp.dot(left, right, preferred_element_type=jnp.float32)


def order_of(tiles, count):
    listed = []
    for tile in range(TILE_DEV):
        hit = jnp.int32(0)
        for slot in range(SLOTS):
            hit = jnp.where((tiles(slot) == tile) & (slot < count), 1, hit)
        listed.append(hit)
    total = functools.reduce(lambda a, b: a + b, listed)
    places = []
    ahead = jnp.int32(0)
    behind = total
    for tile in range(TILE_DEV):
        places.append(jnp.where(listed[tile] == 1, ahead, behind))
        ahead = ahead + listed[tile]
        behind = behind + (1 - listed[tile])
    return places


def place_of(places, tile):
    at = places[0]
    for other in range(1, TILE_DEV):
        at = jnp.where(tile == other, places[other], at)
    return at


def halves_kernel(self_ref, neigh_ref, after_ref, out_ref, buf, sems):
    loads = [pltpu.make_async_copy(ref, buf.at[i], sems.at[i]) for i, ref in enumerate((self_ref, neigh_ref))]
    stores = [pltpu.make_async_copy(buf.at[i % 2], out_ref.at[i], sems.at[2 + i]) for i in range(out_ref.shape[0])]
    for load in loads:
        load.start()
    for kind, load in enumerate(loads):
        load.wait()
        for store in stores[kind::2]:
            store.start()
    for store in stores:
        store.wait()


def far_kernel(
    adj_ref, src_ref, cot_ref, w_ref,
    back_ref, up_ref, down_ref, adj_buf, cot_buf, w_buf, acc_ref, fold_ref, sems,
):
    seeds = adj_ref.shape[0]
    loads = [pltpu.make_async_copy(adj_ref.at[s], adj_buf.at[s], sems.at[s]) for s in range(seeds)]
    load_w = pltpu.make_async_copy(w_ref, w_buf, sems.at[seeds])
    load_cot = pltpu.make_async_copy(cot_ref, cot_buf, sems.at[seeds + 1])
    for load in loads:
        load.start()
    load_cot.start()
    load_w.start()
    acc_ref[...] = jnp.zeros_like(acc_ref)
    for seed in range(seeds):
        loads[seed].wait()
        rows = pl.ds(seed * TILE, TILE)

        def add(k, _):
            slot = src_ref[seed, k] - TILE_DEV
            low = (slot >= 0) & (slot < SLOTS)
            high = slot >= 3 * SLOTS

            @pl.when(low | high)
            def _():
                at = jnp.where(low, slot, slot - 2 * SLOTS)
                cols = pl.ds(pl.multiple_of(at * TILE, TILE), TILE)
                acc_ref[rows, cols] += adj_buf[seed, k].astype(jnp.float32)

            return 0

        lax.fori_loop(0, adj_ref.shape[1], add, 0, unroll=4)
    fold_ref[...] = acc_ref[...].astype(jnp.bfloat16)
    load_cot.wait()
    load_w.wait()
    back = nt_dot(cot_buf[...], w_buf[...]).astype(jnp.bfloat16)
    back_ref[...] = back
    half = SLOTS * TILE
    up_ref[...] = tn_dot(fold_ref[:, :half], back).astype(jnp.bfloat16).reshape(up_ref.shape)
    down_ref[...] = tn_dot(fold_ref[:, half:], back).astype(jnp.bfloat16).reshape(down_ref.shape)


def near_kernel(adj_ref, src_ref, back_ref, fold_ref, far_ref, up_ref, down_ref, acc_ref):
    acc_ref[...] = jnp.zeros_like(acc_ref)
    for seed in range(adj_ref.shape[0]):
        rows = pl.ds(seed * TILE, TILE)

        def add(k, _):
            cols = pl.ds(pl.multiple_of(src_ref[seed, k] * TILE, TILE), TILE)
            acc_ref[rows, cols] += adj_ref[seed, k].astype(jnp.float32)
            return 0

        lax.fori_loop(0, adj_ref.shape[1], add, 0, unroll=4)
    first, half = TILE_DEV * TILE, SLOTS * TILE
    start = first + half
    fold_ref[:, :first] = acc_ref[:, :first].astype(jnp.bfloat16)
    fold_ref[:, first:] = acc_ref[:, start : start + 2 * half].astype(jnp.bfloat16)
    far_ref[:, :half] = acc_ref[:, first:start].astype(jnp.bfloat16)
    far_ref[:, half:] = acc_ref[:, start + 2 * half :].astype(jnp.bfloat16)
    back = back_ref[...]
    up_ref[...] = tn_dot(fold_ref[:, first:start], back).astype(jnp.bfloat16).reshape(up_ref.shape)
    down_ref[...] = tn_dot(fold_ref[:, start:], back).astype(jnp.bfloat16).reshape(down_ref.shape)


def local_kernel(fold_ref, back_ref, cot_ref, w_ref, seeds_ref, after_up_ref, after_down_ref, out_ref):
    rows = out_ref.shape[0]
    back_self = nt_dot(cot_ref[...], w_ref[...]).astype(jnp.bfloat16)
    hot = lax.broadcasted_iota(jnp.int32, (rows, seeds_ref.shape[1]), 0) == seeds_ref[...]
    hot = hot.astype(jnp.float32).astype(jnp.bfloat16)
    out_ref[...] = nn_dot(hot, back_self) + tn_dot(fold_ref[:, :rows], back_ref[...])


def gather_kernel(src_ref, feat_ref, adj_ref, after_ref, out_ref):
    step = pl.program_id(0)
    width = feat_ref.shape[0]
    span = out_ref.shape[2]
    out_ref[0, :width] = feat_ref[:, pl.ds(pl.multiple_of(step * span, span), span)]
    for tile in range(adj_ref.shape[0]):
        parts = []
        for k in range(adj_ref.shape[1]):
            source = src_ref[k, step * adj_ref.shape[0] + tile]
            parts.append(feat_ref[:, pl.ds(pl.multiple_of(source * TILE, TILE), TILE)])
        left = jnp.concatenate(parts, axis=1)
        right = jnp.concatenate([adj_ref[tile, k] for k in range(adj_ref.shape[1])], axis=1)
        out_ref[0, width:, tile * TILE : (tile + 1) * TILE] = nt_dot(left, right).astype(jnp.bfloat16)


def hidden_kernel(
    in_ref, mine_ref, other_ref, bias_ref, odd_ref, tiles_ref, count_ref, after_ref,
    hid_ref, up_ref, down_ref, turned_ref,
):
    slices, width, span = in_ref.shape[0], in_ref.shape[1] // 2, in_ref.shape[2]
    depth = slices * width

    @pl.when(pl.program_id(0) == 0)
    def _():
        for half, odd in enumerate((odd_ref[0], 1 - odd_ref[0])):
            kind = in_ref[:, pl.ds(pl.multiple_of(odd * width, width), width)]
            turned_ref[:, half * depth : (half + 1) * depth] = kind.reshape(depth, span).T

    total = nn_dot(turned_ref[:, :depth], mine_ref[...]) + nn_dot(turned_ref[:, depth:], other_ref[...])
    hidden = jnp.maximum(total + bias_ref[...], 0.0).astype(jnp.bfloat16)
    hid_ref[...] = hidden.reshape(hid_ref.shape)
    shape = (2 * ROWS, up_ref.shape[1])
    row = lax.broadcasted_iota(jnp.int32, shape, 0)
    block = (lax.broadcasted_iota(jnp.int32, shape, 1) + pl.program_id(0) * shape[1]) // TILE
    for near_q, far_q, out_ref in ((2, 3, up_ref), (1, 0, down_ref)):
        places = order_of(lambda m: tiles_ref[far_q, m], count_ref[far_q])
        for tile in range(TILE_DEV):

            @pl.when(places[tile] < NEAR)
            def _():
                at = jnp.minimum(places[tile], NEAR - 1) * TILE
                out_ref[pl.ds(pl.multiple_of(at, TILE), TILE)] = hid_ref[tile]

        marks = jnp.zeros(shape, jnp.float32)
        for first, q in ((0, near_q), (SLOTS, far_q)):
            for slot in range(SLOTS):
                at = jnp.where(slot < count_ref[q], place_of(places, tiles_ref[q, slot]), -1)
                marks = jnp.where((row == first + slot) & (block == at), 1.0, marks)
        out_ref[NEAR * TILE :] = marks.astype(jnp.bfloat16)


def merge_kernel(
    local_ref, from_0_ref, from_1_ref, from_2_ref, from_3_ref, hid_ref, tiles_ref, count_ref,
    out_ref, rest_up_ref, rest_down_ref,
):
    out_ref[...] = local_ref[...]
    for q, ref in enumerate((from_0_ref, from_1_ref, from_2_ref, from_3_ref)):
        for slot in range(SLOTS):

            @pl.when(slot < count_ref[q])
            def _():
                at = pl.multiple_of(tiles_ref[q, slot] * TILE, TILE)
                out_ref[pl.ds(at, TILE)] += ref[slot].astype(jnp.float32)

    for far_q, rest_ref in ((3, rest_up_ref), (0, rest_down_ref)):
        places = order_of(lambda m: tiles_ref[far_q, m], count_ref[far_q])
        for tile in range(TILE_DEV):

            @pl.when(places[tile] >= NEAR)
            def _():
                rest_ref[jnp.maximum(places[tile] - NEAR, 0)] = hid_ref[tile]


def placed(fold_ref, start, mark_ref, first, count, out_ref, to):
    marks = mark_ref[NEAR * TILE :].astype(jnp.float32)
    blocks = [
        fold_ref[:, (start + slot) * TILE : (start + slot + 1) * TILE].astype(jnp.float32) for slot in range(SLOTS)
    ]
    for place in range(count):
        cols = slice(place * TILE, (place + 1) * TILE)
        total = sum(blocks[slot] * marks[first + slot : first + slot + 1, cols] for slot in range(SLOTS))
        out_ref[:, (to + place) * TILE : (to + place + 1) * TILE] = total.astype(jnp.bfloat16)


def mid_kernel(
    fold_ref, hid_ref, a_up_ref, rest_up_ref, a_down_ref, rest_down_ref, seeds_ref, w_ref, bias_ref,
    part_ref, self_ref, placed_ref, table_ref,
):
    rows = TILE_DEV * TILE
    quad = NEAR * TILE
    pair = rows - quad
    hidden = hid_ref[...].reshape(rows, hid_ref.shape[2])
    start = 0
    for first, a_ref, rest_ref in ((TILE_DEV, a_down_ref, rest_down_ref), (TILE_DEV + SLOTS, a_up_ref, rest_up_ref)):
        placed(fold_ref, first, a_ref, 0, TILE_DEV, placed_ref, start // TILE)
        table_ref[start : start + quad] = a_ref[:quad]
        table_ref[start + quad : start + rows] = rest_ref[...].reshape(pair, rest_ref.shape[2])
        start += rows
    part_ref[...] = nn_dot(fold_ref[:, :rows], hidden) + nn_dot(placed_ref[...], table_ref[...])
    hot = lax.broadcasted_iota(jnp.int32, (rows, seeds_ref.shape[1]), 0) == seeds_ref[...]
    hot = hot.astype(jnp.float32).astype(jnp.bfloat16)
    chosen = tn_dot(hot, hidden).astype(jnp.bfloat16)
    self_ref[...] = nn_dot(chosen, w_ref[...]) + bias_ref[...]


def last_kernel(fold_ref, f_up_ref, f_down_ref, part_ref, self_ref, w_ref, out_ref, placed_ref, buf, sems):
    quad = NEAR * TILE
    placed(fold_ref, 0, f_down_ref, SLOTS, NEAR, placed_ref, 0)
    placed(fold_ref, SLOTS, f_up_ref, SLOTS, NEAR, placed_ref, NEAR)
    half = buf.shape[0] // 2
    stores = []
    for part in range(2):
        rows = slice(part * half, (part + 1) * half)
        gathered = part_ref[rows] + nn_dot(placed_ref[rows, :quad], f_down_ref[:quad])
        gathered = (gathered + nn_dot(placed_ref[rows, quad:], f_up_ref[:quad])).astype(jnp.bfloat16)
        buf[rows] = (self_ref[rows] + nn_dot(gathered, w_ref[...])).astype(jnp.bfloat16)
        stores.append(pltpu.make_async_copy(buf.at[rows], out_ref.at[rows], sems.at[part]))
        stores[-1].start()
    for store in stores:
        store.wait()


def shards(
    features,
    adj_one,
    src_one,
    w_self_one,
    w_neigh_one,
    bias_one,
    w_self_two,
    w_neigh_two,
    bias_two,
    seed_rows,
    adj_two,
    src_two,
    send_tiles,
    send_count,
    cotangent,
):
    bf16, f32 = jnp.bfloat16, jnp.float32
    width = features.shape[0]
    part_tiles = adj_one.shape[0]
    hid = w_self_two.shape[0]
    feat_count = lax.axis_size("feat")
    row_dev = features.shape[1] // feat_count
    seeds = cotangent.shape[1]
    blocks, sources = adj_two[0, 0], src_two[0, 0]
    upstream = cotangent[0]
    shape = jax.ShapeDtypeStruct

    lists = send_tiles[0, 0]
    partner = lax.axis_index("dom") + jnp.array(OFFSETS, jnp.int32)
    inside = (partner >= 0) & (partner < lax.axis_size("dom"))
    counts = jnp.where(inside, send_count[0, 0], 0)
    quad = shape((NEAR, TILE, hid), bf16)
    pair = shape((TILE_DEV - NEAR, TILE, hid), bf16)
    quad_marked = shape((NEAR * TILE + 2 * ROWS, hid), bf16)
    far_cols, near_cols = 2 * SLOTS * TILE, (TILE_DEV + 2 * SLOTS) * TILE

    back, far_up, far_down = call(
        far_kernel,
        (shape((seeds, hid), bf16), quad, quad),
        [ANY, SMEM, ANY, ANY],
        [
            pltpu.VMEM(blocks.shape, bf16),
            pltpu.VMEM((seeds, hid), bf16),
            pltpu.VMEM((hid, hid), bf16),
            pltpu.VMEM((seeds, far_cols), f32),
            pltpu.VMEM((seeds, far_cols), bf16),
            pltpu.SemaphoreType.DMA((blocks.shape[0] + 2,)),
        ],
        vmem=56,
            )(blocks, sources, upstream, w_neigh_two)
    halves = call(
        halves_kernel,
        shape((feat_count, width, hid), bf16),
        [ANY, ANY, ANY],
        [pltpu.VMEM((2, width, hid), bf16), pltpu.SemaphoreType.DMA((2 + feat_count,))],
        vmem=56,
        out_specs=ANY,
    )(w_self_one, w_neigh_one, far_up)
    halves = lax.all_to_all(halves, "feat", 0, 0)
    halves = halves.reshape(feat_count * width, hid)
    got_far_up = shifted(far_up, 1)
    got_far_down = shifted(far_down, -1)

    fold_near, fold_far, near_up, near_down = call(
        near_kernel,
        (shape((seeds, near_cols), bf16), shape((seeds, far_cols), bf16), quad, quad),
        [VMEM, SMEM, VMEM],
        [pltpu.VMEM((seeds, near_cols + far_cols), f32)],
        vmem=28,
    )(blocks, sources, back)

    sent = pl.pallas_call(
        gather_kernel,
        grid=(feat_count,),
        in_specs=[
            SMEM,
            pl.BlockSpec((width, features.shape[1]), lambda i: (0, 0)),
            pl.BlockSpec((part_tiles // feat_count,) + adj_one.shape[1:], lambda i: (i, 0, 0, 0)),
            ANY,
        ],
        out_specs=pl.BlockSpec((1, 2 * width, row_dev), lambda i: (i, 0, 0)),
        out_shape=shape((feat_count, 2 * width, row_dev), bf16),
        cost_estimate=pl.CostEstimate(flops=100 * GIGA, bytes_accessed=1, transcendentals=0),
        compiler_params=pltpu.CompilerParams(vmem_limit_bytes=56 * MIB),
    )(src_one.T, features, adj_one, near_up)
    taken = lax.all_to_all(sent, "feat", 0, 0)
    swapped = lax.ppermute(halves, "feat", [(i, i ^ 1) for i in range(feat_count)])
    odd = (lax.axis_index("feat") % 2).astype(jnp.int32)[None]

    grad_1 = shifted(near_up, 1)
    grad_2 = shifted(near_down, -1)
    grad_0 = shifted(got_far_up, 1)
    grad_3 = shifted(got_far_down, -1)

    local = call(
        local_kernel,
        shape((row_dev, hid), f32),
        [VMEM] * 5 + [ANY] * 2,
        cost=20,
        vmem=28,
    )(fold_near, back, upstream, w_self_two, seed_rows[0], got_far_up, got_far_down)

    chunk = hid
    hidden, h_up, h_down = pl.pallas_call(
        hidden_kernel,
        grid=(hid // chunk,),
        in_specs=[
            pl.BlockSpec(taken.shape, lambda j: (0, 0, 0)),
            pl.BlockSpec((feat_count * width, chunk), lambda j: (0, j)),
            pl.BlockSpec((feat_count * width, chunk), lambda j: (0, j)),
            pl.BlockSpec((1, chunk), lambda j: (0, j)),
            SMEM,
            SMEM,
            SMEM,
            ANY,
        ],
        out_specs=[
            pl.BlockSpec((TILE_DEV, TILE, chunk), lambda j: (0, 0, j)),
            pl.BlockSpec((quad_marked.shape[0], chunk), lambda j: (0, j)),
            pl.BlockSpec((quad_marked.shape[0], chunk), lambda j: (0, j)),
        ],
        out_shape=(shape((TILE_DEV, TILE, hid), bf16), quad_marked, quad_marked),
        scratch_shapes=[
            pltpu.VMEM((row_dev, 2 * width * feat_count), bf16),
        ],
        cost_estimate=pl.CostEstimate(flops=GIGA, bytes_accessed=1, transcendentals=0),
        compiler_params=pltpu.CompilerParams(vmem_limit_bytes=30 * MIB),
    )(taken, halves, swapped, bias_one[None], odd, lists, counts, local)
    got_h_up = shifted(h_up, 1)
    got_h_down = shifted(h_down, -1)
    next_up = open_shift(got_h_up, 1)
    next_down = open_shift(got_h_down, -1)
    grads, rest_up, rest_down = call(
        merge_kernel, (shape((row_dev, hid), f32), pair, pair), [VMEM] * 6 + [SMEM] * 2, vmem=24
    )(local, grad_0, grad_1, grad_2, grad_3, hidden, lists, counts)
    got_rest_up = shifted(rest_up, 1)
    got_rest_down = shifted(rest_down, -1)

    part, self_term = call(
        mid_kernel,
        (shape((seeds, hid), f32), shape((seeds, hid), f32)),
        [VMEM] * 9,
        [pltpu.VMEM((seeds, 2 * row_dev), bf16), pltpu.VMEM((2 * row_dev, hid), bf16)],
        cost=100,
        vmem=32,
    )(
        fold_near, hidden, got_h_up, got_rest_up, got_h_down, got_rest_down,
        seed_rows[0], w_self_two, bias_two[None],
    )
    layer_out = call(
        last_kernel,
        shape((seeds, hid), bf16),
        [VMEM] * 6,
        [pltpu.VMEM((seeds, far_cols), bf16), pltpu.VMEM((seeds, hid), bf16), pltpu.SemaphoreType.DMA((2,))],
        out_specs=ANY,
        vmem=20,
    )(fold_far, next_up, next_down, part, self_term, w_neigh_two)
    return (layer_out[None], grads[None])


def solution(mesh):
    return jax.shard_map(
        shards,
        mesh=mesh,
        in_specs=(
            P("feat", "dom"),
            P("dom", None, None, None),
            P("dom", None),
            P("feat", None),
            P("feat", None),
            P(),
            P(),
            P(),
            P(),
            P("dom", "feat", None),
            P("dom", "feat", None, None, None, None),
            P("dom", "feat", None, None),
            P("dom", "feat", None, None),
            P("dom", "feat", None),
            P("dom", "feat", None),
        ),
        out_specs=(P("dom", "feat", None), P("dom", "feat", None)),
        check_vma=False,
    )
```

```python
import functools

import jax
import jax.numpy as jnp
from jax import lax
from jax.experimental import pallas as pl
from jax.experimental.pallas import tpu as pltpu
from jax.sharding import PartitionSpec as P

TILE = 128
TILE_DEV = 6
SLOTS = 4
NEAR = 4
ROWS = 8
MIB = 1 << 20
OFFSETS = (-2, -1, 1, 2)
GIGA = 1 << 30

VMEM = pl.BlockSpec(memory_space=pltpu.VMEM)
SMEM = pl.BlockSpec(memory_space=pltpu.SMEM)
ANY = pl.BlockSpec(memory_space=pl.ANY)


def open_shift(shard, by):
    count = lax.axis_size("dom")
    return lax.ppermute(shard, "dom", [(i, i + by) for i in range(count) if 0 <= i + by < count])


def shifted(shard, by):
    count = lax.axis_size("dom")
    return lax.ppermute(shard, "dom", [(i, (i + by) % count) for i in range(count)])


def call(body, outs, in_specs, scratch=(), cost=1, vmem=32, out_specs=None):
    return pl.pallas_call(
        body,
        out_shape=outs,
        in_specs=in_specs,
        out_specs=out_specs or jax.tree.map(lambda _: VMEM, outs),
        scratch_shapes=list(scratch),
        cost_estimate=pl.CostEstimate(flops=cost * GIGA, bytes_accessed=1, transcendentals=0),
        compiler_params=pltpu.CompilerParams(vmem_limit_bytes=vmem * MIB),
    )


def tn_dot(left, right):
    return lax.dot_general(left, right, (((0,), (0,)), ((), ())), preferred_element_type=jnp.float32)


def nt_dot(left, right):
    return lax.dot_general(left, right, (((1,), (1,)), ((), ())), preferred_element_type=jnp.float32)


def nn_dot(left, right):
    return jnp.dot(left, right, preferred_element_type=jnp.float32)


def order_of(tiles, count):
    listed = []
    for tile in range(TILE_DEV):
        hit = jnp.int32(0)
        for slot in range(SLOTS):
            hit = jnp.where((tiles(slot) == tile) & (slot < count), 1, hit)
        listed.append(hit)
    total = functools.reduce(lambda a, b: a + b, listed)
    places = []
    ahead = jnp.int32(0)
    behind = total
    for tile in range(TILE_DEV):
        places.append(jnp.where(listed[tile] == 1, ahead, behind))
        ahead = ahead + listed[tile]
        behind = behind + (1 - listed[tile])
    return places


def place_of(places, tile):
    at = places[0]
    for other in range(1, TILE_DEV):
        at = jnp.where(tile == other, places[other], at)
    return at


def halves_kernel(self_ref, neigh_ref, after_ref, out_ref, buf, sems):
    loads = [pltpu.make_async_copy(ref, buf.at[i], sems.at[i]) for i, ref in enumerate((self_ref, neigh_ref))]
    stores = [pltpu.make_async_copy(buf.at[i % 2], out_ref.at[i], sems.at[2 + i]) for i in range(out_ref.shape[0])]
    for load in loads:
        load.start()
    for kind, load in enumerate(loads):
        load.wait()
        for store in stores[kind::2]:
            store.start()
    for store in stores:
        store.wait()


def far_kernel(
    adj_ref, src_ref, cot_ref, w_ref,
    back_ref, fold_ref, up_ref, down_ref, adj_buf, cot_buf, w_buf, acc_ref, sems,
):
    seeds = adj_ref.shape[0]
    loads = [pltpu.make_async_copy(adj_ref.at[s], adj_buf.at[s], sems.at[s]) for s in range(seeds)]
    load_w = pltpu.make_async_copy(w_ref, w_buf, sems.at[seeds])
    load_cot = pltpu.make_async_copy(cot_ref, cot_buf, sems.at[seeds + 1])
    for load in loads:
        load.start()
    load_cot.start()
    load_w.start()
    acc_ref[...] = jnp.zeros_like(acc_ref)
    for seed in range(seeds):
        loads[seed].wait()
        rows = pl.ds(seed * TILE, TILE)

        def add(k, _):
            slot = src_ref[seed, k] - TILE_DEV
            low = (slot >= 0) & (slot < SLOTS)
            high = slot >= 3 * SLOTS

            @pl.when(low | high)
            def _():
                at = jnp.where(low, slot, slot - 2 * SLOTS)
                cols = pl.ds(pl.multiple_of(at * TILE, TILE), TILE)
                acc_ref[rows, cols] += adj_buf[seed, k].astype(jnp.float32)

            return 0

        lax.fori_loop(0, adj_ref.shape[1], add, 0, unroll=4)
    fold_ref[...] = acc_ref[...].astype(jnp.bfloat16)
    load_cot.wait()
    load_w.wait()
    back = nt_dot(cot_buf[...], w_buf[...]).astype(jnp.bfloat16)
    back_ref[...] = back
    half = SLOTS * TILE
    up_ref[...] = tn_dot(fold_ref[:, :half], back).astype(jnp.bfloat16).reshape(up_ref.shape)
    down_ref[...] = tn_dot(fold_ref[:, half:], back).astype(jnp.bfloat16).reshape(down_ref.shape)


def near_kernel(adj_ref, src_ref, back_ref, fold_ref, up_ref, down_ref, acc_ref):
    acc_ref[...] = jnp.zeros_like(acc_ref)
    for seed in range(adj_ref.shape[0]):
        rows = pl.ds(seed * TILE, TILE)

        def add(k, _):
            slot = src_ref[seed, k]
            local = slot < TILE_DEV
            near = (slot >= TILE_DEV + SLOTS) & (slot < TILE_DEV + 3 * SLOTS)

            @pl.when(local | near)
            def _():
                at = jnp.where(local, slot, slot - SLOTS)
                cols = pl.ds(pl.multiple_of(at * TILE, TILE), TILE)
                acc_ref[rows, cols] += adj_ref[seed, k].astype(jnp.float32)

            return 0

        lax.fori_loop(0, adj_ref.shape[1], add, 0, unroll=4)
    fold_ref[...] = acc_ref[...].astype(jnp.bfloat16)
    back = back_ref[...]
    start, half = TILE_DEV * TILE, SLOTS * TILE
    up_ref[...] = tn_dot(fold_ref[:, start : start + half], back).astype(jnp.bfloat16).reshape(up_ref.shape)
    down_ref[...] = tn_dot(fold_ref[:, start + half :], back).astype(jnp.bfloat16).reshape(down_ref.shape)


def local_kernel(fold_ref, back_ref, cot_ref, w_ref, seeds_ref, after_up_ref, after_down_ref, out_ref):
    rows = out_ref.shape[0]
    back_self = nt_dot(cot_ref[...], w_ref[...]).astype(jnp.bfloat16)
    hot = lax.broadcasted_iota(jnp.int32, (rows, seeds_ref.shape[1]), 0) == seeds_ref[...]
    hot = hot.astype(jnp.float32).astype(jnp.bfloat16)
    out_ref[...] = nn_dot(hot, back_self) + tn_dot(fold_ref[:, :rows], back_ref[...])


def gather_kernel(src_ref, feat_ref, adj_ref, after_ref, out_ref):
    step = pl.program_id(0)
    width = feat_ref.shape[0]
    span = out_ref.shape[2]
    out_ref[0, :width] = feat_ref[:, pl.ds(pl.multiple_of(step * span, span), span)]
    for tile in range(adj_ref.shape[0]):
        parts = []
        for k in range(adj_ref.shape[1]):
            source = src_ref[k, step * adj_ref.shape[0] + tile]
            parts.append(feat_ref[:, pl.ds(pl.multiple_of(source * TILE, TILE), TILE)])
        left = jnp.concatenate(parts, axis=1)
        right = jnp.concatenate([adj_ref[tile, k] for k in range(adj_ref.shape[1])], axis=1)
        out_ref[0, width:, tile * TILE : (tile + 1) * TILE] = nt_dot(left, right).astype(jnp.bfloat16)


def hidden_kernel(
    in_ref, mine_ref, other_ref, bias_ref, odd_ref, tiles_ref, count_ref, after_ref,
    hid_ref, up_ref, down_ref, turned_ref,
):
    slices, width, span = in_ref.shape[0], in_ref.shape[1] // 2, in_ref.shape[2]
    depth = slices * width

    @pl.when(pl.program_id(0) == 0)
    def _():
        for half, odd in enumerate((odd_ref[0], 1 - odd_ref[0])):
            kind = in_ref[:, pl.ds(pl.multiple_of(odd * width, width), width)]
            turned_ref[:, half * depth : (half + 1) * depth] = kind.reshape(depth, span).T

    total = nn_dot(turned_ref[:, :depth], mine_ref[...]) + nn_dot(turned_ref[:, depth:], other_ref[...])
    hidden = jnp.maximum(total + bias_ref[...], 0.0).astype(jnp.bfloat16)
    hid_ref[...] = hidden.reshape(hid_ref.shape)
    shape = (2 * ROWS, up_ref.shape[1])
    row = lax.broadcasted_iota(jnp.int32, shape, 0)
    block = (lax.broadcasted_iota(jnp.int32, shape, 1) + pl.program_id(0) * shape[1]) // TILE
    for near_q, far_q, out_ref in ((2, 3, up_ref), (1, 0, down_ref)):
        places = order_of(lambda m: tiles_ref[far_q, m], count_ref[far_q])
        for tile in range(TILE_DEV):

            @pl.when(places[tile] < NEAR)
            def _():
                at = jnp.minimum(places[tile], NEAR - 1) * TILE
                out_ref[pl.ds(pl.multiple_of(at, TILE), TILE)] = hid_ref[tile]

        marks = jnp.zeros(shape, jnp.float32)
        for first, q in ((0, near_q), (SLOTS, far_q)):
            for slot in range(SLOTS):
                at = jnp.where(slot < count_ref[q], place_of(places, tiles_ref[q, slot]), -1)
                marks = jnp.where((row == first + slot) & (block == at), 1.0, marks)
        out_ref[NEAR * TILE :] = marks.astype(jnp.bfloat16)


def merge_kernel(
    local_ref, from_0_ref, from_1_ref, from_2_ref, from_3_ref, hid_ref, tiles_ref, count_ref,
    out_ref, rest_up_ref, rest_down_ref,
):
    out_ref[...] = local_ref[...]
    for q, ref in enumerate((from_0_ref, from_1_ref, from_2_ref, from_3_ref)):
        for slot in range(SLOTS):

            @pl.when(slot < count_ref[q])
            def _():
                at = pl.multiple_of(tiles_ref[q, slot] * TILE, TILE)
                out_ref[pl.ds(at, TILE)] += ref[slot].astype(jnp.float32)

    for far_q, rest_ref in ((3, rest_up_ref), (0, rest_down_ref)):
        places = order_of(lambda m: tiles_ref[far_q, m], count_ref[far_q])
        for tile in range(TILE_DEV):

            @pl.when(places[tile] >= NEAR)
            def _():
                rest_ref[jnp.maximum(places[tile] - NEAR, 0)] = hid_ref[tile]


def placed(fold_ref, start, mark_ref, first, count, out_ref, to):
    marks = mark_ref[NEAR * TILE :].astype(jnp.float32)
    blocks = [
        fold_ref[:, (start + slot) * TILE : (start + slot + 1) * TILE].astype(jnp.float32) for slot in range(SLOTS)
    ]
    for place in range(count):
        cols = slice(place * TILE, (place + 1) * TILE)
        total = sum(blocks[slot] * marks[first + slot : first + slot + 1, cols] for slot in range(SLOTS))
        out_ref[:, (to + place) * TILE : (to + place + 1) * TILE] = total.astype(jnp.bfloat16)


def mid_kernel(
    fold_ref, hid_ref, a_up_ref, rest_up_ref, a_down_ref, rest_down_ref, seeds_ref, w_ref, bias_ref,
    part_ref, self_ref, placed_ref, table_ref,
):
    rows = TILE_DEV * TILE
    quad = NEAR * TILE
    pair = rows - quad
    hidden = hid_ref[...].reshape(rows, hid_ref.shape[2])
    start = 0
    for first, a_ref, rest_ref in ((TILE_DEV, a_down_ref, rest_down_ref), (TILE_DEV + SLOTS, a_up_ref, rest_up_ref)):
        placed(fold_ref, first, a_ref, 0, TILE_DEV, placed_ref, start // TILE)
        table_ref[start : start + quad] = a_ref[:quad]
        table_ref[start + quad : start + rows] = rest_ref[...].reshape(pair, rest_ref.shape[2])
        start += rows
    part_ref[...] = nn_dot(fold_ref[:, :rows], hidden) + nn_dot(placed_ref[...], table_ref[...])
    hot = lax.broadcasted_iota(jnp.int32, (rows, seeds_ref.shape[1]), 0) == seeds_ref[...]
    hot = hot.astype(jnp.float32).astype(jnp.bfloat16)
    chosen = tn_dot(hot, hidden).astype(jnp.bfloat16)
    self_ref[...] = nn_dot(chosen, w_ref[...]) + bias_ref[...]


def last_kernel(fold_ref, f_up_ref, f_down_ref, part_ref, self_ref, w_ref, out_ref, placed_ref):
    quad = NEAR * TILE
    placed(fold_ref, 0, f_down_ref, SLOTS, NEAR, placed_ref, 0)
    placed(fold_ref, SLOTS, f_up_ref, SLOTS, NEAR, placed_ref, NEAR)
    gathered = part_ref[...] + nn_dot(placed_ref[:, :quad], f_down_ref[:quad])
    gathered = (gathered + nn_dot(placed_ref[:, quad:], f_up_ref[:quad])).astype(jnp.bfloat16)
    out_ref[...] = (self_ref[...] + nn_dot(gathered, w_ref[...])).astype(jnp.bfloat16)


def shards(
    features,
    adj_one,
    src_one,
    w_self_one,
    w_neigh_one,
    bias_one,
    w_self_two,
    w_neigh_two,
    bias_two,
    seed_rows,
    adj_two,
    src_two,
    send_tiles,
    send_count,
    cotangent,
):
    bf16, f32 = jnp.bfloat16, jnp.float32
    width = features.shape[0]
    part_tiles = adj_one.shape[0]
    hid = w_self_two.shape[0]
    feat_count = lax.axis_size("feat")
    row_dev = features.shape[1] // feat_count
    seeds = cotangent.shape[1]
    blocks, sources = adj_two[0, 0], src_two[0, 0]
    upstream = cotangent[0]
    shape = jax.ShapeDtypeStruct

    lists = send_tiles[0, 0]
    partner = lax.axis_index("dom") + jnp.array(OFFSETS, jnp.int32)
    inside = (partner >= 0) & (partner < lax.axis_size("dom"))
    counts = jnp.where(inside, send_count[0, 0], 0)
    quad = shape((NEAR, TILE, hid), bf16)
    pair = shape((TILE_DEV - NEAR, TILE, hid), bf16)
    quad_marked = shape((NEAR * TILE + 2 * ROWS, hid), bf16)
    far_cols, near_cols = 2 * SLOTS * TILE, (TILE_DEV + 2 * SLOTS) * TILE

    back, fold_far, far_up, far_down = call(
        far_kernel,
        (shape((seeds, hid), bf16), shape((seeds, far_cols), bf16), quad, quad),
        [ANY, SMEM, ANY, ANY],
        [
            pltpu.VMEM(blocks.shape, bf16),
            pltpu.VMEM((seeds, hid), bf16),
            pltpu.VMEM((hid, hid), bf16),
            pltpu.VMEM((seeds, far_cols), f32),
            pltpu.SemaphoreType.DMA((blocks.shape[0] + 2,)),
        ],
        vmem=56,
            )(blocks, sources, upstream, w_neigh_two)
    halves = call(
        halves_kernel,
        shape((feat_count, width, hid), bf16),
        [ANY, ANY, ANY],
        [pltpu.VMEM((2, width, hid), bf16), pltpu.SemaphoreType.DMA((2 + feat_count,))],
        vmem=56,
        out_specs=ANY,
    )(w_self_one, w_neigh_one, far_up)
    halves = lax.all_to_all(halves, "feat", 0, 0)
    halves = halves.reshape(feat_count * width, hid)
    got_far_up = shifted(far_up, 1)
    got_far_down = shifted(far_down, -1)

    fold_near, near_up, near_down = call(
        near_kernel,
        (shape((seeds, near_cols), bf16), quad, quad),
        [VMEM, SMEM, VMEM],
        [pltpu.VMEM((seeds, near_cols), f32)],
        vmem=24,
    )(blocks, sources, back)

    sent = pl.pallas_call(
        gather_kernel,
        grid=(feat_count,),
        in_specs=[
            SMEM,
            pl.BlockSpec((width, features.shape[1]), lambda i: (0, 0)),
            pl.BlockSpec((part_tiles // feat_count,) + adj_one.shape[1:], lambda i: (i, 0, 0, 0)),
            ANY,
        ],
        out_specs=pl.BlockSpec((1, 2 * width, row_dev), lambda i: (i, 0, 0)),
        out_shape=shape((feat_count, 2 * width, row_dev), bf16),
        cost_estimate=pl.CostEstimate(flops=100 * GIGA, bytes_accessed=1, transcendentals=0),
        compiler_params=pltpu.CompilerParams(vmem_limit_bytes=40 * MIB),
    )(src_one.T, features, adj_one, near_up)
    taken = lax.all_to_all(sent, "feat", 0, 0)
    swapped = lax.ppermute(halves, "feat", [(i, i ^ 1) for i in range(feat_count)])
    odd = (lax.axis_index("feat") % 2).astype(jnp.int32)[None]

    grad_1 = shifted(near_up, 1)
    grad_2 = shifted(near_down, -1)
    grad_0 = shifted(got_far_up, 1)
    grad_3 = shifted(got_far_down, -1)

    local = call(
        local_kernel,
        shape((row_dev, hid), f32),
        [VMEM] * 5 + [ANY] * 2,
        cost=20,
        vmem=28,
    )(fold_near, back, upstream, w_self_two, seed_rows[0], got_far_up, got_far_down)

    chunk = hid
    hidden, h_up, h_down = pl.pallas_call(
        hidden_kernel,
        grid=(hid // chunk,),
        in_specs=[
            pl.BlockSpec(taken.shape, lambda j: (0, 0, 0)),
            pl.BlockSpec((feat_count * width, chunk), lambda j: (0, j)),
            pl.BlockSpec((feat_count * width, chunk), lambda j: (0, j)),
            pl.BlockSpec((1, chunk), lambda j: (0, j)),
            SMEM,
            SMEM,
            SMEM,
            ANY,
        ],
        out_specs=[
            pl.BlockSpec((TILE_DEV, TILE, chunk), lambda j: (0, 0, j)),
            pl.BlockSpec((quad_marked.shape[0], chunk), lambda j: (0, j)),
            pl.BlockSpec((quad_marked.shape[0], chunk), lambda j: (0, j)),
        ],
        out_shape=(shape((TILE_DEV, TILE, hid), bf16), quad_marked, quad_marked),
        scratch_shapes=[
            pltpu.VMEM((row_dev, 2 * width * feat_count), bf16),
        ],
        cost_estimate=pl.CostEstimate(flops=GIGA, bytes_accessed=1, transcendentals=0),
        compiler_params=pltpu.CompilerParams(vmem_limit_bytes=30 * MIB),
    )(taken, halves, swapped, bias_one[None], odd, lists, counts, local)
    got_h_up = shifted(h_up, 1)
    got_h_down = shifted(h_down, -1)
    next_up = open_shift(got_h_up, 1)
    next_down = open_shift(got_h_down, -1)
    grads, rest_up, rest_down = call(
        merge_kernel, (shape((row_dev, hid), f32), pair, pair), [VMEM] * 6 + [SMEM] * 2, vmem=24
    )(local, grad_0, grad_1, grad_2, grad_3, hidden, lists, counts)
    got_rest_up = shifted(rest_up, 1)
    got_rest_down = shifted(rest_down, -1)

    part, self_term = call(
        mid_kernel,
        (shape((seeds, hid), f32), shape((seeds, hid), f32)),
        [VMEM] * 9,
        [pltpu.VMEM((seeds, 2 * row_dev), bf16), pltpu.VMEM((2 * row_dev, hid), bf16)],
        cost=100,
        vmem=32,
    )(
        fold_near, hidden, got_h_up, got_rest_up, got_h_down, got_rest_down,
        seed_rows[0], w_self_two, bias_two[None],
    )
    layer_out = call(
        last_kernel,
        shape((seeds, hid), bf16),
        [VMEM] * 6,
        [pltpu.VMEM((seeds, far_cols), bf16)],
        vmem=20,
    )(fold_far, next_up, next_down, part, self_term, w_neigh_two)
    return (layer_out[None], grads[None])


def solution(mesh):
    return jax.shard_map(
        shards,
        mesh=mesh,
        in_specs=(
            P("feat", "dom"),
            P("dom", None, None, None),
            P("dom", None),
            P("feat", None),
            P("feat", None),
            P(),
            P(),
            P(),
            P(),
            P("dom", "feat", None),
            P("dom", "feat", None, None, None, None),
            P("dom", "feat", None, None),
            P("dom", "feat", None, None),
            P("dom", "feat", None),
            P("dom", "feat", None),
        ),
        out_specs=(P("dom", "feat", None), P("dom", "feat", None)),
        check_vma=False,
    )
```
